128 devices in a mesh: prompt: 8 (over z_hi, x), roll: 16 (over y, z_lo, core).
Axes of the slice: x: 4, y: 4, z: 4 (z_hi: 2, z_lo: 2; z = z_hi * 2 + z_lo), core: 2. Of those that a mesh axis runs over, the one named last changes fastest.
Arguments:
- prompt_cache: bfloat16 [16, 1024, 512], P('prompt', 'roll'), may hold values from -12 to 12
- key_gain: float32 [128], replicated, may hold values from 1 to 2
- query_gain: float32 [128], replicated, may hold values from 1 to 2
- window_cache: bfloat16 [256, 128, 512], P(('prompt', 'roll')), may hold values from -12 to 12
- queries: bfloat16 [256, 128, 4096], P(('prompt', 'roll')), may hold values from -6 to 6
- upstream: bfloat16 [256, 128, 4096], P(('prompt', 'roll')), may hold values from -6 to 6
- rewards: float32 [256], P(('prompt', 'roll')), may hold values from 0 to 3
- assign: int32 [256], P(('prompt', 'roll')), may hold values from 0 to 1, as said below
- offsets: int32 [256], P(('prompt', 'roll')), may hold values from 0 to 3968
Outputs:
- attended: bfloat16 [256, 128, 4096], P(('prompt', 'roll'))
- query_grad: bfloat16 [256, 128, 4096], P(('prompt', 'roll'))
- window_grad: bfloat16 [256, 128, 512], P(('prompt', 'roll'))
- prompt_grad: bfloat16 [16, 1024, 512], P('prompt', 'roll')
The draws below stay inside these ranges and needn't reach their ends.
Inputs may be any that keep to these rules, and one draw needn't show every extreme that they name: `assign`: within each group of 32 rollouts, each of the 2 prompt indices is named by exactly 16 rollouts.
All inputs are finite; a program needn't handle non-finite values.
Results may differ from the reference program's by a relative error of at most 0.023.
Values may be sent and summed in bfloat16 or wider, within the bound.
No kernel may reach another device: no remote copies, remote signals or barrier semaphores. Data moves between devices by JAX's collectives and lax.ppermute only.
A program may use at most 192 MiB of HBM per device.

```python
import math
import jax
import jax.numpy as jnp
from jax import lax

HD = 128
QH = 32
KVH = 2
WIN = 128
PLEN = 1024
RESP = 4096
PG = 2
PROMPTS = 16
GROUP_ROLLS = 32
ROLLS = 256


def draw_assign(key, part):
    key = jax.random.fold_in(key, 11)
    group_keys = jax.random.split(key, ROLLS // GROUP_ROLLS)

    def one_group(single):
        return jax.random.permutation(single, GROUP_ROLLS)
    orders = jax.vmap(one_group)(group_keys)
    return (orders % PG).reshape(ROLLS).astype(jnp.int32)


def draw_rewards(key, part):
    key = jax.random.fold_in(key, 5)
    rising = 1.0 + 2.0 * jnp.arange(ROLLS, dtype=jnp.float32) / (ROLLS - 1)
    base = jax.random.uniform(key, (ROLLS,), jnp.float32)
    return base * rising


def place_ends(entries, rng, smallest, largest):
    extent = entries.shape
    place = [jax.random.randint(jax.random.fold_in(rng, axis), (), 0, extent[axis]) for axis in range(len(extent))]
    entries = entries.at[tuple(place)].set(smallest)
    longest = extent.index(max(extent))
    place[longest] = (place[longest] + 1) % extent[longest]
    return entries.at[tuple(place)].set(largest)


def levels(key, shape, cuts, smallest, high):
    def one(dim, blocks):
        heights = jax.random.uniform(jax.random.fold_in(jax.random.fold_in(key, 6), dim), (blocks,), jnp.float32, smallest / len(cuts), high / len(cuts))
        return jnp.repeat(jnp.exp(heights), shape[dim] // blocks).reshape((-1,) + (1,) * (len(shape) - dim - 1))

    level = one(*cuts[0])
    for cut in cuts[1:]:
        level = level * one(*cut)
    return level


def gaussian(rng, shape, spread, limit, pieces=(), held_as=jnp.bfloat16):
    entries = jax.random.normal(rng, shape, jnp.float32) * spread
    if len(pieces) > 0:
        entries = levels(rng, shape, pieces, -0.22, 0.18) * entries
    return jnp.clip(entries, min=-limit, max=limit).astype(held_as)


def setup_inputs(seed: int = 0) -> dict:
    seeds = jax.random.split(jax.random.key(seed), 10)
    prompt_cache = gaussian(seeds[0], (PROMPTS, PLEN, 2 * KVH * HD), 2.0, 12.0, ((0, 8), (1, 16)))
    key_gain = jnp.clip(jax.random.uniform(seeds[1], (HD,), jnp.float32, 1.0, 2.0), 1.0, 2.0)
    query_gain = jnp.clip(jax.random.uniform(seeds[2], (HD,), jnp.float32, 1.0, 2.0), 1.0, 2.0)
    window_cache = gaussian(seeds[3], (ROLLS, WIN, 2 * KVH * HD), 2.0, 12.0, ((0, 128),))
    queries = gaussian(seeds[4], (ROLLS, WIN, QH * HD), 1.0, 6.0, ((0, 128),))
    upstream = gaussian(seeds[5], (ROLLS, WIN, QH * HD), 1.0, 6.0, ((0, 128),))
    rewards = draw_rewards(jax.random.fold_in(seeds[9], 71), 0)
    assign = draw_assign(jax.random.fold_in(seeds[9], 71), 0)
    offsets = place_ends(jax.random.randint(seeds[8], (ROLLS,), 0, RESP - WIN + 1), jax.random.fold_in(seeds[8], 1), 0, RESP - WIN).astype(jnp.int32)
    return {"prompt_cache": prompt_cache, "key_gain": key_gain, "query_gain": query_gain, "window_cache": window_cache, "queries": queries, "upstream": upstream, "rewards": rewards, "assign": assign, "offsets": offsets}


rope_base = 1000000.0
norm_eps = 1e-06
spread_eps = 1e-06

def rotate(values, positions):
    half_size = values.shape[-1] // 2
    frequency = rope_base ** (-(jnp.arange(half_size, dtype=jnp.float32) * 2.0) / values.shape[-1])
    angles = positions.astype(jnp.float32)[:, None] * frequency[None, :]
    cosine = jnp.cos(angles)[:, None, :]
    sine_part = jnp.sin(angles)[:, None, :]
    lower_half = values[..., :half_size]
    upper_half = values[..., half_size:]
    return jnp.concatenate([lower_half * cosine - upper_half * sine_part, upper_half * cosine + lower_half * sine_part], axis=-1)

def prepare(values, gain, positions):
    inverse = lax.rsqrt(lax.optimization_barrier(jnp.mean(values * values, axis=-1, keepdims=True)) + norm_eps)
    return rotate(values * inverse * gain, positions)

def rounded(values):
    return lax.optimization_barrier(values.astype(jnp.bfloat16)).astype(jnp.float32)

def reference(prompt_cache, key_gain, query_gain, window_cache, queries, upstream, rewards, assign, offsets):
    key_width = KVH * HD
    group_size = QH // KVH
    root_size = math.sqrt(HD)
    group_index = jnp.arange(ROLLS, dtype=jnp.int32) // GROUP_ROLLS
    prompt_index = group_index * PG + assign
    member = (prompt_index[:, None] == jnp.arange(PROMPTS, dtype=jnp.int32)[None, :]).astype(jnp.float32)
    prompt_means = lax.optimization_barrier(jnp.sum(member * rewards[:, None], axis=0)) / (GROUP_ROLLS // PG)
    centred = rewards - lax.optimization_barrier(jnp.sum(member * prompt_means[None, :], axis=1))
    advantage = centred / jnp.sqrt(jnp.mean(centred * centred) + spread_eps)
    prompt_pos = jnp.arange(PLEN, dtype=jnp.int32)
    raw_keys = prompt_cache[:, :, :key_width].astype(jnp.float32).reshape(PROMPTS, PLEN, KVH, HD)

    def prompt_prepare(features):
        return prepare(features, key_gain, prompt_pos)
    ready_keys = rounded(jax.vmap(prompt_prepare)(raw_keys))
    prompt_values = prompt_cache[:, :, key_width:].astype(jnp.float32).reshape(PROMPTS, PLEN, KVH, HD)
    token_index = jnp.arange(WIN, dtype=jnp.int32)
    key_index = jnp.arange(PLEN + WIN, dtype=jnp.int32)
    visible = (key_index[None, :] < PLEN) | (key_index[None, :] - PLEN <= token_index[:, None])

    def one_rollout(totals, rollout):
        chosen = prompt_index[rollout].astype(jnp.int32)
        positions = PLEN + offsets[rollout] + token_index

        def query_prepare(features):
            return prepare(features, query_gain, positions)

        def window_prepare(features):
            return prepare(features, key_gain, positions)
        raw_query = queries[rollout].astype(jnp.float32).reshape(WIN, QH, HD)
        ready_query = rounded(query_prepare(raw_query))
        raw_window = window_cache[rollout][:, :key_width].astype(jnp.float32).reshape(WIN, KVH, HD)
        window_keys = rounded(window_prepare(raw_window))
        window_values = window_cache[rollout][:, key_width:].astype(jnp.float32).reshape(WIN, KVH, HD)
        all_keys = jnp.concatenate([lax.dynamic_index_in_dim(ready_keys, chosen, 0, keepdims=False), window_keys], axis=0)
        all_values = jnp.concatenate([lax.dynamic_index_in_dim(prompt_values, chosen, 0, keepdims=False), window_values], axis=0)
        grouped = ready_query.reshape(WIN, KVH, group_size, HD).transpose(1, 2, 0, 3)
        scores = jnp.einsum('hgid,thd->hgit', grouped, all_keys) / root_size
        exponent = jnp.where(visible[None, None], jnp.exp(scores), 0.0)
        denominator = lax.optimization_barrier(jnp.sum(exponent, axis=-1))
        weights = rounded(exponent)
        numerator = jnp.einsum('hgit,thd->hgid', weights, all_values)
        output = numerator / denominator[..., None]
        attended = output.transpose(2, 0, 1, 3).reshape(WIN, QH * HD).astype(jnp.bfloat16)
        grad_out = rounded(advantage[rollout] * upstream[rollout].astype(jnp.float32))
        grad_out = grad_out.reshape(WIN, KVH, group_size, HD).transpose(1, 2, 0, 3)
        row_dot = lax.optimization_barrier(jnp.sum(grad_out * output, axis=-1))
        normed_prob = exponent / denominator[..., None]
        grad_prob = jnp.einsum('hgid,thd->hgit', grad_out, all_values)
        grad_score = rounded(normed_prob * (grad_prob - row_dot[..., None]))
        rounded_prob = rounded(normed_prob)
        grad_query = jnp.einsum('hgit,thd->hgid', grad_score, all_keys) / root_size
        grad_keys = jnp.einsum('hgit,hgid->thd', grad_score, grouped) / root_size
        grad_values = jnp.einsum('hgit,hgid->thd', rounded_prob, grad_out)
        grad_query = grad_query.transpose(2, 0, 1, 3).reshape(WIN, QH, HD)
        query_pull = jax.vjp(query_prepare, raw_query)[1]
        query_grad = query_pull(grad_query)[0].reshape(WIN, QH * HD).astype(jnp.bfloat16)
        window_pull = jax.vjp(window_prepare, raw_window)[1]
        window_key_grad = window_pull(grad_keys[PLEN:])[0].reshape(WIN, key_width)
        window_grad = jnp.concatenate([window_key_grad, grad_values[PLEN:].reshape(WIN, key_width)], axis=1).astype(jnp.bfloat16)
        prompt_part = jnp.concatenate([grad_keys[:PLEN].reshape(PLEN, key_width), grad_values[:PLEN].reshape(PLEN, key_width)], axis=1)
        anchor = jnp.zeros((), jnp.int32)
        previous = lax.dynamic_slice(totals, (chosen, anchor, anchor), (1, PLEN, 2 * key_width))
        totals = lax.dynamic_update_slice(totals, previous + prompt_part[None], (chosen, anchor, anchor))
        return (totals, (attended, query_grad, window_grad))
    totals = jnp.zeros((PROMPTS, PLEN, 2 * key_width), jnp.float32)
    totals, outputs = lax.scan(one_rollout, totals, jnp.arange(ROLLS, dtype=jnp.int32))
    attended, query_grad, window_grad = outputs
    prompt_pull = jax.vjp(jax.vmap(prompt_prepare), raw_keys)[1]
    prompt_key_grad = prompt_pull(totals[:, :, :key_width].reshape(PROMPTS, PLEN, KVH, HD))[0].reshape(PROMPTS, PLEN, key_width)
    prompt_grad = jnp.concatenate([prompt_key_grad, totals[:, :, key_width:]], axis=2).astype(jnp.bfloat16)
    return (attended, query_grad, window_grad, prompt_grad)
```

```python
import functools
import math

import jax
import jax.numpy as jnp
from jax import lax
from jax.experimental import pallas as pl
from jax.experimental.pallas import tpu as pltpu
from jax.sharding import PartitionSpec as P

rope_base = 1000000.0
norm_eps = 1e-06
spread_eps = 1e-06
LOG2E = math.log2(math.e)
bf16, f32 = jnp.bfloat16, jnp.float32


def dot(a, b, ca, cb):
    return lax.dot_general(a, b, (((ca,), (cb,)), ((), ())), preferred_element_type=f32)


def helpers():
    i = lax.broadcasted_iota(jnp.int32, (128, 128), 0)
    j = lax.broadcasted_iota(jnp.int32, (128, 128), 1)
    swap = ((i == j + 64) | (j == i + 64)).astype(bf16)
    mean = jnp.full((128, 128), 1.0 / 128, bf16)
    return swap, mean


def unit(raw, mean):
    v = raw.astype(f32)
    return lax.rsqrt(dot((v * v).astype(bf16), mean, 1, 0) + norm_eps)


def prepare(raw, gain, rgain, cos, sin, swap, mean):
    inv = unit(raw, mean)
    u = raw.astype(f32) * inv * gain
    ru = dot(raw, swap, 1, 0) * inv * rgain
    return u * cos + ru * sin, ru * cos - u * sin


def pull(raw, g, rg, gain, cos, sin, mean):
    v = raw.astype(f32)
    inv = unit(raw, mean)
    gw = (g * cos - rg * sin) * gain
    return inv * (gw - v * (inv * inv * dot((gw * v).astype(bf16), mean, 1, 0)))


def attend(
    assign, q_ref, up_ref, ga_ref, gb_ref, wk_ref, wv_ref, qg_ref, kg_ref, cp_ref, sp_ref, cw_ref, sw_ref,
    w_ref, adv_ref, *refs, heads, subs, plen, chips, tok, win,
):
    att_ref, dq_ref, dw_ref, own_ref, oth_ref, kp, va, dk, dv = refs[-9:]
    r, hb = pl.program_id(0), pl.program_id(1)
    root = math.sqrt(128)
    half = plen // 2
    swap, mean = helpers()
    kgain, qgain = kg_ref[...], qg_ref[...]
    rkgain, rqgain = pltpu.roll(kgain, 64, 1), pltpu.roll(qgain, 64, 1)

    @pl.when(hb == 0)
    def _():
        for i, g_ref in enumerate((ga_ref, gb_ref)):
            raw = g_ref[:, 0].reshape(half, 256)
            rows = pl.ds(i * half, half)
            k, rk = prepare(raw[:, :128], kgain, rkgain, cp_ref[rows, :], sp_ref[rows, :], swap, mean)
            kp[rows, :128] = k.astype(bf16)
            kp[rows, 128:] = rk.astype(bf16)
            va[rows, :128] = raw[:, 128:]
        k, rk = prepare(wk_ref[0], kgain, rkgain, cw_ref[0], sw_ref[0], swap, mean)
        kp[plen:, :128] = k.astype(bf16)
        kp[plen:, 128:] = rk.astype(bf16)
        va[plen:, :128] = wv_ref[0]
        va[:, 128:] = jnp.ones_like(va[:, 128:])
        dk[r] = jnp.zeros_like(dk[r])
        dv[r] = jnp.zeros_like(dv[r])

    sh = heads // subs
    cos = jnp.concatenate([cw_ref[0]] * sh, axis=0)
    sin = jnp.concatenate([sw_ref[0]] * sh, axis=0)
    rows = sh * win
    i = lax.broadcasted_iota(jnp.int32, (rows, win), 0) % win
    j = lax.broadcasted_iota(jnp.int32, (rows, win), 1)
    seen = i >= j
    S = range(subs)

    def load(ref, b):
        return jnp.concatenate([ref[0, :, (b * sh + g) * 128 : (b * sh + g + 1) * 128] for g in range(sh)], axis=0)

    def store(ref, b, x):
        for g in range(sh):
            ref[0, :, (b * sh + g) * 128 : (b * sh + g + 1) * 128] = x[g * win : (g + 1) * win]

    q = [load(q_ref, b) for b in S]
    qc = LOG2E / root
    qs = [prepare(q[b], qgain * qc, rqgain * qc, cos, sin, swap, mean)[0].astype(bf16) for b in S]
    s = [dot(qs[b], kp[:, :128], 1, 1) for b in S]
    e = [jnp.exp2(s[b]) for b in S]
    e = [jnp.concatenate([e[b][:, :plen], jnp.where(seen, e[b][:, plen:], 0.0)], axis=1).astype(bf16) for b in S]
    od = [dot(e[b], va[...], 1, 0) for b in S]
    a = []
    for b in S:
        rinv = 1.0 / od[b][:, 128:]
        o = od[b][:, :128] * rinv
        store(att_ref, b, o.astype(bf16))
        do = load(up_ref, b).astype(f32) * rinv
        a.append(jnp.concatenate([do.astype(bf16), (-(do * o)).astype(bf16)], axis=1))
    dp = [dot(a[b], va[...], 1, 1) for b in S]
    ds = [e[b] * dp[b].astype(bf16) for b in S]
    gq = [dot(ds[b], kp[...], 1, 0) for b in S]
    for b in S:
        store(dq_ref, b, pull(q[b], gq[b][:, :128], gq[b][:, 128:], qgain * (adv_ref[r] / root), cos, sin, mean).astype(bf16))
    cat = lambda x: jnp.concatenate(x, axis=0) if subs > 1 else x[0]
    dv[r] += dot(cat(a)[:, :128], cat(e), 0, 0)
    dk[r] += dot(cat(qs), cat(ds), 0, 0)

    @pl.when(hb == pl.num_programs(1) - 1)
    def _():
        ln2 = 1.0 / LOG2E
        gk = dk[r, :, plen:].T * (ln2 * adv_ref[r])
        dw_ref[0, :, :128] = pull(wk_ref[0], gk, pltpu.roll(gk, 64, 1), kgain, cw_ref[0], sw_ref[0], mean).astype(bf16)
        dw_ref[0, :, 128:] = (dv[r, :, plen:].T * adv_ref[r]).astype(bf16)

        @pl.when(r == 1)
        def _():
            for i, out in enumerate((own_ref, oth_ref)):
                cols = pl.ds(i * half, half)
                for p in range(2):
                    for c, (acc, scale) in enumerate(((dk, ln2), (dv, 1.0))):
                        m = (w_ref[p, 0] * scale) * acc[0, :, cols] + (w_ref[p, 1] * scale) * acc[1, :, cols]
                        out[:, p, :, c * 128 : (c + 1) * 128] = m.astype(bf16).T.reshape(chips, tok, 128)


def call(h, heads, subs, assign, q, up, ga, gb, wc, qgain, kgain, cp, sp, cw, sw, w, adv, *before):
    rolls, win, width = q.shape
    chips, prompts, tok, _ = ga.shape
    kvh = wc.shape[2] // 256
    share = width // (128 * kvh)
    plen = 2 * chips * tok
    steps = share // heads
    t = plen + win
    smem = pl.BlockSpec(memory_space=pltpu.SMEM)
    anywhere = pl.BlockSpec(memory_space=pl.ANY)
    vec = pl.BlockSpec((1, 128), lambda r, b, a: (0, 0))
    gspec = pl.BlockSpec((chips, 1, tok, 256), lambda r, b, a: (0, a[r], 0, 0))
    qspec = pl.BlockSpec((1, win, heads * 128), lambda r, b, a: (r, 0, h * steps + b))
    pspec = pl.BlockSpec((plen, 128), lambda r, b, a: (0, 0))
    wspec = pl.BlockSpec((1, win, 128), lambda r, b, a: (r, 0, 0))
    pieces = pl.BlockSpec((chips, prompts, tok, 256), lambda r, b, a: (0, 0, 0, 0))
    return pl.pallas_call(
        functools.partial(attend, heads=heads, subs=subs, plen=plen, chips=chips, tok=tok, win=win),
        grid_spec=pltpu.PrefetchScalarGridSpec(
            num_scalar_prefetch=1,
            grid=(rolls, steps),
            in_specs=[
                qspec,
                qspec,
                gspec,
                gspec,
                pl.BlockSpec((1, win, 128), lambda r, b, a: (r, 0, h)),
                pl.BlockSpec((1, win, 128), lambda r, b, a: (r, 0, kvh + h)),
                vec,
                vec,
                pspec,
                pspec,
                wspec,
                wspec,
                smem,
                smem,
            ]
            + [anywhere] * len(before),
            out_specs=[qspec, qspec, pl.BlockSpec((1, win, 256), lambda r, b, a: (r, 0, 0)), pieces, pieces],
            scratch_shapes=[
                pltpu.VMEM((t, 256), bf16),
                pltpu.VMEM((t, 256), bf16),
                pltpu.VMEM((rolls, 128, t), f32),
                pltpu.VMEM((rolls, 128, t), f32),
            ],
        ),
        out_shape=[
            jax.ShapeDtypeStruct(q.shape, bf16),
            jax.ShapeDtypeStruct(q.shape, bf16),
            jax.ShapeDtypeStruct((rolls, win, 256), bf16),
            jax.ShapeDtypeStruct((chips, prompts, tok, 256), bf16),
            jax.ShapeDtypeStruct((chips, prompts, tok, 256), bf16),
        ],
        input_output_aliases={15: 0, 16: 1} if before else {},
        compiler_params=pltpu.CompilerParams(vmem_limit_bytes=56 * 1024 * 1024),
        cost_estimate=pl.CostEstimate(
            flops=12 * rolls * share * win * t * 128, bytes_accessed=8 * rolls * share * win * 128, transcendentals=rolls * share * win * t
        ),
        name="attend",
    )(assign, q, up, ga, gb, wc, wc, qgain, kgain, cp, sp, cw, sw, w, adv, *before)


def tables(positions):
    frequency = rope_base ** (-(jnp.arange(64, dtype=f32) * 2.0) / 128)
    angles = positions.astype(f32)[..., None] * frequency
    c, s = jnp.cos(angles), jnp.sin(angles)
    return jnp.concatenate([c, c], axis=-1), jnp.concatenate([-s, s], axis=-1)


def local(prompt_cache, key_gain, query_gain, window_cache, queries, upstream, rewards, assign, offsets):
    groups, members = lax.axis_size("prompt"), lax.axis_size("roll")
    rolls, win, width = queries.shape
    prompts, tok, _ = prompt_cache.shape
    kvh = window_cache.shape[2] // 256
    chips = members // 2
    devices = groups * members
    mine = lax.axis_index("roll")
    core = mine % 2
    same_core = [[2 * c + k for c in range(chips)] for k in range(2)]
    other_core = [(m, m ^ 1) for m in range(members)]

    def flip(x):
        return lax.ppermute(x, "roll", other_core)

    def exchange(x):
        return lax.all_to_all(x, "roll", 0, 0, tiled=True, axis_index_groups=same_core)

    sent = []
    for h in range(kvh):
        part = jnp.concatenate(
            [prompt_cache[:, :, h * 128 : (h + 1) * 128], prompt_cache[:, :, (kvh + h) * 128 : (kvh + h + 1) * 128]], axis=2
        )
        sent.append(exchange(jnp.broadcast_to(part[None], (chips,) + part.shape)))
    facts = jnp.concatenate([rewards, assign.astype(f32), jnp.zeros((128 - 2 * rolls,), f32)])
    facts = lax.all_to_all(jnp.broadcast_to(facts, (devices, 1, 128)), ("prompt", "roll"), 0, 0, tiled=True)[:, 0]
    held = [(g, flip(g)) for g in sent]

    all_rewards = facts[:, :rolls].reshape(-1)
    group = jnp.arange(devices * rolls) // (members * rolls)
    prompt_of = group * prompts + facts[:, rolls : 2 * rolls].reshape(-1).astype(jnp.int32)
    member = (prompt_of[:, None] == jnp.arange(groups * prompts)[None, :]).astype(f32)
    per_prompt = rolls * members // prompts
    means = jnp.sum(member * all_rewards[:, None], axis=0) / per_prompt
    centred = all_rewards - jnp.sum(member * means[None, :], axis=1)
    spread = jnp.sum(centred * centred) / (devices * rolls)
    here = (lax.axis_index("prompt") * members + mine) * rolls
    adv = lax.dynamic_slice(centred, (here,), (rolls,)) / jnp.sqrt(spread + spread_eps)
    w = (assign[None, :] == jnp.arange(prompts, dtype=jnp.int32)[:, None]).astype(f32) * adv[None, :]

    token = jnp.arange(tok)
    chip = jnp.arange(chips)[:, None]
    spots = jnp.stack([(chip * 2 + core) * tok + token, (chip * 2 + 1 - core) * tok + token]).reshape(-1)
    cp, sp = tables(spots)
    cw, sw = tables(2 * chips * tok + offsets[:, None] + jnp.arange(win)[None, :])
    qgain, kgain = query_gain[None], key_gain[None]

    before, window_parts, reduced = [], [], []
    for h in range(kvh):
        att, dq, dw, own, other = call(
            h, 8, 2, assign, queries, upstream, held[h][0], held[h][1], window_cache, qgain, kgain, cp, sp, cw, sw, w, adv, *before
        )
        before = [att, dq]
        window_parts.append(dw)
        merged = (own.astype(f32) + flip(other).astype(f32)).astype(bf16)
        reduced.append(jnp.sum(exchange(merged).astype(f32), axis=0))

    co, so = tables(mine * tok + token)
    raw = jnp.concatenate([prompt_cache[:, :, None, h * 128 : (h + 1) * 128] for h in range(kvh)], axis=2).astype(f32)
    g = jnp.stack([x[:, :, :128] for x in reduced], axis=2)
    co, so = co[None, :, None], so[None, :, None]
    inv = lax.rsqrt(jnp.mean(raw * raw, axis=-1, keepdims=True) + norm_eps)
    gw = (g * co - jnp.roll(g, 64, axis=-1) * so) * key_gain
    gk = inv * (gw - raw * (inv * inv * jnp.mean(gw * raw, axis=-1, keepdims=True)))
    prompt_grad = jnp.concatenate([gk.reshape(prompts, tok, kvh * 128)] + [x[:, :, 128:] for x in reduced], axis=2).astype(bf16)
    window_grad = jnp.concatenate([x[:, :, :128] for x in window_parts] + [x[:, :, 128:] for x in window_parts], axis=2)
    return att, dq, window_grad, prompt_grad


def solution(mesh):
    both = P(("prompt", "roll"))
    return jax.shard_map(
        local,
        mesh=mesh,
        in_specs=(P("prompt", "roll", None), P(), P(), both, both, both, both, both, both),
        out_specs=(both, both, both, P("prompt", "roll", None)),
        check_vma=False,
    )
```

```python
import functools
import math

import jax
import jax.numpy as jnp
import numpy as np
from jax import lax
from jax.experimental import pallas as pl
from jax.experimental.pallas import tpu as pltpu
from jax.sharding import PartitionSpec as P

rope_base = 1000000.0
norm_eps = 1e-06
spread_eps = 1e-06
LOG2E = math.log2(math.e)
bf16, f32 = jnp.bfloat16, jnp.float32
LIMIT = 56 * 1024 * 1024
frequency = np.tile(rope_base ** (-np.arange(64) * 2.0 / 128), 2).astype(np.float32)[None]


def dot(a, b, ca, cb):
    return lax.dot_general(a, b, (((ca,), (cb,)), ((), ())), preferred_element_type=f32)


def helpers():
    i = lax.broadcasted_iota(jnp.int32, (128, 128), 0)
    j = lax.broadcasted_iota(jnp.int32, (128, 128), 1)
    swap = ((i == j + 64) | (j == i + 64)).astype(bf16)
    mean = jnp.full((128, 128), 1.0 / 128, bf16)
    return swap, mean


def unit(raw, mean):
    v = raw.astype(f32)
    return lax.rsqrt(dot((v * v).astype(bf16), mean, 1, 0) + norm_eps)


def prepare(raw, gain, cos, sin, swap, mean):
    inv = unit(raw, mean)
    u = raw.astype(f32) * inv * gain
    ru = dot(raw, swap, 1, 0) * inv * pltpu.roll(gain, 64, 1)
    return u * cos + ru * sin, ru * cos - u * sin


def pull(raw, g, rg, gain, cos, sin, mean):
    v = raw.astype(f32)
    inv = unit(raw, mean)
    gw = (g * cos - rg * sin) * gain
    return inv * (gw - v * (inv * inv * dot((gw * v).astype(bf16), mean, 1, 0)))


def turns(start, count, freq):
    positions = (start + lax.broadcasted_iota(jnp.int32, (count, 128), 0)).astype(f32)
    angles = positions * freq
    upper = lax.broadcasted_iota(jnp.int32, (count, 128), 1) >= 64
    sine = jnp.sin(angles)
    return jnp.cos(angles), jnp.where(upper, sine, -sine)


def ready(q_ref, gain_ref, freq_ref, off_ref, qs_ref, cw_ref, sw_ref, *, heads, plen):
    swap, mean = helpers()
    gain = gain_ref[...] * (LOG2E / math.sqrt(128))
    win = cw_ref.shape[1]
    cw, sw = turns(plen + off_ref[pl.program_id(0)], win, freq_ref[...])
    cw_ref[0] = cw
    sw_ref[0] = sw
    cos, sin = (jnp.concatenate([x] * heads, axis=0) for x in (cw, sw))
    q = jnp.concatenate([q_ref[0, :, g * 128 : (g + 1) * 128] for g in range(heads)], axis=0)
    qs_ref[0] = prepare(q, gain, cos, sin, swap, mean)[0].astype(bf16).reshape(heads, win, 128)


def attend(
    scalar, qs_ref, q_ref, up_ref, ga_ref, gb_ref, fa_ref, fb_ref, wk_ref, wv_ref, qg_ref, kg_ref, cw_ref, sw_ref, rw_ref, *refs,
    heads, subs, tc, merge, tok, win
):
    n_out = 4 + (1 if merge else 2)
    att_ref, dq_ref, dwin_ref, stat_ref, *outs = refs[-6 - n_out : -6]
    kp, va, dk, dv, e_ref, ds_ref = refs[-6:]
    r, hb = pl.program_id(0), pl.program_id(1)
    core = scalar[2]
    chips = ga_ref.shape[0]
    half = chips * tok
    plen = 2 * half
    t = plen + win
    root = math.sqrt(128)
    kgain = kg_ref[...]
    swap, mean = helpers()

    @pl.when(hb == 0)
    def _():
        for i, g_ref in enumerate((ga_ref, gb_ref)):
            raw = g_ref[...].reshape(half, 256)
            rows = pl.ds(i * half, half)
            kp[rows, :128] = raw[:, :128]
            kp[rows, 128:] = dot(raw[:, :128], swap, 1, 0).astype(bf16)
            va[rows, :128] = raw[:, 128:]
        k, rk = prepare(wk_ref[0], kgain, cw_ref[0], sw_ref[0], swap, mean)
        kp[plen:, :128] = k.astype(bf16)
        kp[plen:, 128:] = rk.astype(bf16)
        va[plen:, :128] = wv_ref[0]
        va[:, 128:] = jnp.ones_like(va[:, 128:])
        dk[r] = jnp.zeros_like(dk[r])
        dv[r] = jnp.zeros_like(dv[r])

    sh = heads // subs
    rows = sh * win
    i = lax.broadcasted_iota(jnp.int32, (rows, win), 0) % win
    j = lax.broadcasted_iota(jnp.int32, (rows, win), 1)
    seen = i >= j
    S = range(subs)
    chunks = [slice(c, min(c + tc, plen)) for c in range(0, plen, tc)] + [slice(plen, t)]
    block = [slice(b * rows, (b + 1) * rows) for b in S]
    qs = [qs_ref[0, b * sh : (b + 1) * sh].reshape(rows, 128) for b in S]
    for b in S:
        for c in chunks:
            e = jnp.exp2(dot(qs[b], kp[c, :128], 1, 1))
            if c.start == plen:
                e = jnp.where(seen, e, 0.0)
            e_ref[block[b], c] = e.astype(bf16)
    od = [dot(e_ref[block[b]], va[...], 1, 0) for b in S]
    a = []
    for b in S:
        rinv = 1.0 / od[b][:, 128:]
        o = od[b][:, :128] * rinv
        ob = o.astype(bf16)
        up = []
        for g in range(sh):
            cols = slice((b * sh + g) * 128, (b * sh + g + 1) * 128)
            att_ref[0, :, cols] = ob[g * win : (g + 1) * win]
            up.append(up_ref[0, :, cols])
        do = jnp.concatenate(up, axis=0).astype(f32) * rinv
        a.append(jnp.concatenate([do.astype(bf16), (-(do * o)).astype(bf16)], axis=1))
    for b in S:
        for c in chunks:
            ds_ref[block[b], c] = e_ref[block[b], c] * dot(a[b], va[c], 1, 1).astype(bf16)
    gq = [dot(ds_ref[block[b]], kp[...], 1, 0) for b in S]
    cos, sin = (jnp.concatenate([x[0]] * sh, axis=0) for x in (cw_ref, sw_ref))
    for b in S:
        q = jnp.concatenate([q_ref[0, :, (b * sh + g) * 128 : (b * sh + g + 1) * 128] for g in range(sh)], axis=0)
        dq = pull(q, gq[b][:, :128], gq[b][:, 128:], qg_ref[...] * (1.0 / root), cos, sin, mean).astype(bf16)
        for g in range(sh):
            dq_ref[0, :, (b * sh + g) * 128 : (b * sh + g + 1) * 128] = dq[g * win : (g + 1) * win]
    cat = lambda x: jnp.concatenate(x, axis=0) if subs > 1 else x[0]
    dv[r] += dot(cat(a)[:, :128], e_ref[...], 0, 0)
    dk[r] += dot(cat(qs), ds_ref[...], 0, 0)

    @pl.when(hb == pl.num_programs(1) - 1)
    def _():
        ln2 = 1.0 / LOG2E
        gk = dk[r, :, plen:].T * ln2
        dwin_ref[0, :, :128] = pull(wk_ref[0], gk, pltpu.roll(gk, 64, 1), kgain, cw_ref[0], sw_ref[0], mean)
        dwin_ref[0, :, 128:] = dv[r, :, plen:].T

        @pl.when(r == 1)
        def _():
            f = jnp.concatenate([fa_ref[:, 0], fb_ref[:, 0]], axis=0).astype(f32)
            reward = [f[:, 3 * n : 3 * n + 1] + f[:, 3 * n + 1 : 3 * n + 2] + f[:, 3 * n + 2 : 3 * n + 3] for n in range(2)]
            place = [f[:, 6 + n : 7 + n] for n in range(2)]
            per_prompt = f.shape[0]
            means = [
                sum(jnp.sum(jnp.where(place[n] == p, reward[n], 0.0), axis=0, keepdims=True) for n in range(2)) / per_prompt
                for p in range(2)
            ]
            spread = sum(
                jnp.sum((reward[n] - jnp.where(place[n] == 0, means[0], means[1])) ** 2, axis=0, keepdims=True) for n in range(2)
            )
            centred = [rw_ref[n] - jnp.where(scalar[n] == 0, means[0], means[1]) for n in range(2)]
            lane = lax.broadcasted_iota(jnp.int32, stat_ref.shape, 1)
            stat_ref[...] = jnp.where(lane == 0, spread, jnp.where(lane == 1, centred[0], centred[1]))
            for i in range(2):
                cols = pl.ds(i * half, half)
                for p in range(2):
                    for c, (acc, scale) in enumerate(((dk, ln2), (dv, 1.0))):
                        w = [jnp.where(scalar[n] == p, centred[n], 0.0) * scale for n in range(2)]
                        m = (w[0] * acc[0, :, cols] + w[1] * acc[1, :, cols]).astype(bf16).T.reshape(chips, tok, 128)
                        if merge:
                            outs[0][:, lax.rem(core + i, 2), p, :, c * 128 : (c + 1) * 128] = m
                        else:
                            outs[i][:, p, :, c * 128 : (c + 1) * 128] = m


def call(h, heads, subs, tc, merge, scalar, qs, q, up, ga, gb, fa, fb, wc, qgain, kgain, cw, sw, rewards, tok, prompts, *before):
    rolls, win, width = up.shape
    chips = ga.shape[0]
    kvh = wc.shape[2] // 256
    share = width // (128 * kvh)
    half = chips * tok
    plen = 2 * half
    steps = share // heads
    t = plen + win
    smem = pl.BlockSpec(memory_space=pltpu.SMEM)
    anywhere = pl.BlockSpec(memory_space=pl.ANY)
    if ga.ndim == 3:
        gspecs = [pl.BlockSpec((chips, tok, 256), lambda r, b, a: (0, a[r], 0))] * 2
    else:
        gspecs = [
            pl.BlockSpec((chips, 1, 1, tok, 256), lambda r, b, a: (0, a[2], a[r], 0, 0)),
            pl.BlockSpec((chips, 1, 1, tok, 256), lambda r, b, a: (0, 1 - a[2], a[r], 0, 0)),
        ]
    fspec = pl.BlockSpec((chips, 16, 256), lambda r, b, a: (0, prompts * tok // 16, 0))
    ospec = pl.BlockSpec((1, win, heads * 128), lambda r, b, a: (r, 0, h * steps + b))
    vec = pl.BlockSpec((1, 128), lambda r, b, a: (0, 0))
    wspec = pl.BlockSpec((1, win, 128), lambda r, b, a: (r, 0, 0))
    piece = (chips, 2, prompts, tok, 256) if merge else (chips, prompts, tok, 256)
    pieces = pl.BlockSpec(piece, lambda r, b, a: (0,) * len(piece))
    return pl.pallas_call(
        functools.partial(attend, heads=heads, subs=subs, tc=tc, merge=merge, tok=tok, win=win),
        grid_spec=pltpu.PrefetchScalarGridSpec(
            num_scalar_prefetch=1,
            grid=(rolls, steps),
            in_specs=[
                pl.BlockSpec((1, heads, win, 128), lambda r, b, a: (r, h * steps + b, 0, 0)),
                ospec,
                ospec,
                *gspecs,
                fspec,
                fspec,
                pl.BlockSpec((1, win, 128), lambda r, b, a: (r, 0, h)),
                pl.BlockSpec((1, win, 128), lambda r, b, a: (r, 0, kvh + h)),
                vec,
                vec,
                wspec,
                wspec,
                smem,
            ]
            + [anywhere] * len(before),
            out_specs=[
                ospec,
                ospec,
                pl.BlockSpec((1, win, 256), lambda r, b, a: (r, 0, 0)),
                pl.BlockSpec((8, 128), lambda r, b, a: (0, 0)),
            ]
            + [pieces] * (1 if merge else 2),
            scratch_shapes=[
                pltpu.VMEM((t, 256), bf16),
                pltpu.VMEM((t, 256), bf16),
                pltpu.VMEM((rolls, 128, t), f32),
                pltpu.VMEM((rolls, 128, t), f32),
                pltpu.VMEM((heads * win, t), bf16),
                pltpu.VMEM((heads * win, t), bf16),
            ],
        ),
        out_shape=[
            jax.ShapeDtypeStruct(up.shape, bf16),
            jax.ShapeDtypeStruct(up.shape, bf16),
            jax.ShapeDtypeStruct((rolls, win, 256), f32),
            jax.ShapeDtypeStruct((8, 128), f32),
        ]
        + [jax.ShapeDtypeStruct(piece, bf16)] * (1 if merge else 2),
        input_output_aliases={15: 0, 16: 1} if before else {},
        compiler_params=pltpu.CompilerParams(vmem_limit_bytes=LIMIT),
        cost_estimate=pl.CostEstimate(
            flops=36 * rolls * share * win * t * 128, bytes_accessed=10 * rolls * share * win * 128, transcendentals=rolls * share * win * t
        ),
        name="attend",
    )(scalar, qs, q, up, ga, gb, fa, fb, wc, wc, qgain, kgain, cw, sw, rewards, *before)


def make_ready(q, gain, offsets, plen):
    rolls, win, width = q.shape
    heads = width // 128
    wspec = pl.BlockSpec((1, win, 128), lambda r: (r, 0, 0))
    vec = pl.BlockSpec((1, 128), lambda r: (0, 0))
    return pl.pallas_call(
        functools.partial(ready, heads=heads, plen=plen),
        grid=(rolls,),
        in_specs=[pl.BlockSpec((1, win, width), lambda r: (r, 0, 0)), vec, vec, pl.BlockSpec(memory_space=pltpu.SMEM)],
        out_specs=[pl.BlockSpec((1, heads, win, 128), lambda r: (r, 0, 0, 0)), wspec, wspec],
        out_shape=[jax.ShapeDtypeStruct((rolls, heads, win, 128), bf16)] + [jax.ShapeDtypeStruct((rolls, win, 128), f32)] * 2,
        compiler_params=pltpu.CompilerParams(vmem_limit_bytes=LIMIT),
        name="ready",
    )(q, gain, frequency, offsets)


def pack(cache_ref, reward_ref, assign_ref, kg_ref, freq_ref, mine_ref, first_ref, second_ref):
    prompts, tok, width = cache_ref.shape
    kvh = width // 256
    lane = lax.broadcasted_iota(jnp.int32, (16, 256), 1)
    facts = jnp.zeros((16, 256), f32)
    for n in range(2):
        rest = jnp.full((16, 256), reward_ref[n], f32)
        for k in range(3):
            piece = rest.astype(bf16).astype(f32)
            facts = jnp.where(lane == 3 * n + k, piece, facts)
            rest = rest - piece
        facts = jnp.where(lane == 6 + n, assign_ref[n].astype(f32), facts)
    swap, mean = helpers()
    cos, sin = turns(mine_ref[0] * tok, tok, freq_ref[...])
    order = [(p, h) for p in range(prompts) for h in range(kvh)]
    raw = jnp.concatenate([cache_ref[p, :, h * 128 : (h + 1) * 128] for p, h in order], axis=0)
    cos, sin = (jnp.concatenate([x] * len(order), axis=0) for x in (cos, sin))
    keys = prepare(raw, kg_ref[...], cos, sin, swap, mean)[0].astype(bf16)
    for n, (p, h) in enumerate(order):
        key, value = keys[n * tok : (n + 1) * tok], cache_ref[p, :, (kvh + h) * 128 : (kvh + h + 1) * 128]
        if h == 0:
            for c in range(first_ref.shape[0]):
                first_ref[c, p * tok : (p + 1) * tok, :128] = key
                first_ref[c, p * tok : (p + 1) * tok, 128:] = value
        else:
            second_ref[p, :, :128] = key
            second_ref[p, :, 128:] = value
    for c in range(first_ref.shape[0]):
        first_ref[c, prompts * tok :] = facts.astype(bf16)


def make_pack(cache, rewards, assign, kgain, mine, chips):
    prompts, tok, _ = cache.shape
    smem, vmem = pl.BlockSpec(memory_space=pltpu.SMEM), pl.BlockSpec(memory_space=pltpu.VMEM)
    return pl.pallas_call(
        pack,
        in_specs=[vmem, smem, smem, vmem, vmem, smem],
        out_specs=[vmem, vmem],
        out_shape=[jax.ShapeDtypeStruct((chips, prompts * tok + 16, 256), bf16), jax.ShapeDtypeStruct((prompts, tok, 256), bf16)],
        name="pack",
    )(cache, rewards, assign, kgain, frequency, mine)


def global_scale(sums_ref, count):
    return 1.0 / jnp.sqrt(sums_ref[0:1, 0:1] / count + spread_eps)


def rescale(dq_ref, dw0_ref, dw1_ref, sums_ref, stat_ref, dq_out, dw_out, *, count):
    r = pl.program_id(0)
    adv = jnp.where(r == 0, stat_ref[0:1, 1:2], stat_ref[0:1, 2:3]) * global_scale(sums_ref, count)
    dq_out[...] = (dq_ref[...].astype(f32) * adv).astype(bf16)
    for n, part in enumerate((dw0_ref, dw1_ref)):
        for c in range(2):
            dw_out[0, :, (2 * c + n) * 128 : (2 * c + n + 1) * 128] = (part[0, :, c * 128 : (c + 1) * 128] * adv).astype(bf16)


def make_rescale(dq, dw0, dw1, sums, stat, count):
    rolls, win, width = dq.shape
    half = pl.BlockSpec((1, win, 256), lambda r, b: (r, 0, 0))
    qspec = pl.BlockSpec((1, win, width // 2), lambda r, b: (r, 0, b))
    return pl.pallas_call(
        functools.partial(rescale, count=count),
        grid=(rolls, 2),
        in_specs=[
            qspec,
            half,
            half,
            pl.BlockSpec((8, 128), lambda r, b: (0, 0)),
            pl.BlockSpec((8, 128), lambda r, b: (0, 0)),
        ],
        out_specs=[qspec, pl.BlockSpec((1, win, 512), lambda r, b: (r, 0, 0))],
        out_shape=[jax.ShapeDtypeStruct(dq.shape, bf16), jax.ShapeDtypeStruct((rolls, win, 512), bf16)],
        input_output_aliases={0: 0},
        compiler_params=pltpu.CompilerParams(vmem_limit_bytes=LIMIT),
        name="rescale",
    )(dq, dw0, dw1, sums, stat)


def settle(d0_ref, d1_ref, cache_ref, kg_ref, freq_ref, mine_ref, sums_ref, out_ref, *, count):
    prompts, tok, width = cache_ref.shape
    scale = global_scale(sums_ref, count)
    _, mean = helpers()
    cos, sin = turns(mine_ref[0] * tok, tok, freq_ref[...])
    for h, d_ref in enumerate((d0_ref, d1_ref)):
        for p in range(prompts):
            g = d_ref[0, p].astype(f32)
            for m in range(1, d_ref.shape[0]):
                g += d_ref[m, p].astype(f32)
            g *= scale
            key = pull(cache_ref[p, :, h * 128 : (h + 1) * 128], g[:, :128], pltpu.roll(g[:, :128], 64, 1), kg_ref[...], cos, sin, mean)
            out_ref[p, :, h * 128 : (h + 1) * 128] = key.astype(bf16)
            out_ref[p, :, (2 + h) * 128 : (3 + h) * 128] = g[:, 128:].astype(bf16)


def make_settle(d0, d1, cache, kgain, mine, sums, count):
    smem, vmem = pl.BlockSpec(memory_space=pltpu.SMEM), pl.BlockSpec(memory_space=pltpu.VMEM)
    return pl.pallas_call(
        functools.partial(settle, count=count),
        grid=(1,),
        in_specs=[vmem, vmem, vmem, vmem, vmem, smem, vmem],
        out_specs=vmem,
        out_shape=jax.ShapeDtypeStruct(cache.shape, bf16),
        compiler_params=pltpu.CompilerParams(vmem_limit_bytes=LIMIT),
        name="settle",
    )(d0, d1, cache, kgain, frequency, mine, sums)


def local(prompt_cache, key_gain, query_gain, window_cache, queries, upstream, rewards, assign, offsets):
    groups, members = lax.axis_size("prompt"), lax.axis_size("roll")
    rolls = queries.shape[0]
    prompts, tok, _ = prompt_cache.shape
    chips = members // 2
    mine = lax.axis_index("roll")
    same_core = [[2 * c + k for c in range(chips)] for k in range(2)]
    other_core = [(m, m ^ 1) for m in range(members)]

    def flip(x):
        return lax.ppermute(x, "roll", other_core)

    mine = mine.astype(jnp.int32)[None]
    qgain, kgain = query_gain[None], key_gain[None]
    first, second = make_pack(prompt_cache, rewards, assign, kgain, mine, chips)
    ga = lax.all_to_all(first, "roll", 0, 0, tiled=True, axis_index_groups=same_core)
    scalar = jnp.concatenate([assign, mine % 2])
    qs, cw, sw = make_ready(queries, qgain, offsets, members * tok)
    ga, qs, cw, sw, scalar = lax.optimization_barrier((ga, qs, cw, sw, scalar))
    gb = flip(ga)
    second, _ = lax.optimization_barrier((second, ga))
    g1 = lax.all_to_all(jnp.broadcast_to(second, (members,) + second.shape), "roll", 0, 0, tiled=True).reshape(chips, 2, prompts, tok, 256)

    def add_far(x, step):
        return x + lax.ppermute(x, "prompt", [(i, i ^ step) for i in range(groups)])

    def attention(h, merge, a, b, *before):
        return call(
            h, 16, 4, 512, merge, scalar, qs, queries, upstream, a, b, ga, gb, window_cache, qgain, kgain, cw, sw, rewards, tok, prompts, *before
        )

    att, dq, dw0, stat, pieces = attention(0, True, ga, gb)
    pieces, g1 = lax.optimization_barrier((pieces, g1))
    sum0 = lax.all_to_all(pieces.reshape(members, prompts, tok, 256), "roll", 0, 0, tiled=True)
    sums = add_far(stat, 1)
    att, dq, dw1, _, own, other = attention(1, False, g1, g1, att, dq)
    own, other, sum0, sums = lax.optimization_barrier((own, other, sum0, sums))
    merged = (own.astype(f32) + flip(other).astype(f32)).astype(bf16)
    sums = add_far(sums, 2)
    sum1 = lax.all_to_all(merged, "roll", 0, 0, tiled=True, axis_index_groups=same_core)
    sums, _ = lax.optimization_barrier((sums, merged))
    sums = add_far(sums, 4)
    count = groups * members * rolls
    dq, window_grad = make_rescale(dq, dw0, dw1, sums, stat, count)
    prompt_grad = make_settle(sum0, sum1, prompt_cache, kgain, mine, sums, count)
    return att, dq, window_grad, prompt_grad


def solution(mesh):
    both = P(("prompt", "roll"))
    return jax.shard_map(
        local,
        mesh=mesh,
        in_specs=(P("prompt", "roll", None), P(), P(), both, both, both, both, both, both),
        out_specs=(both, both, both, P("prompt", "roll", None)),
        check_vma=False,
    )
```

```python
import functools
import math

import jax
import jax.numpy as jnp
import numpy as np
from jax import lax
from jax.experimental import pallas as pl
from jax.experimental.pallas import tpu as pltpu
from jax.sharding import PartitionSpec as P

rope_base = 1000000.0
norm_eps = 1e-06
spread_eps = 1e-06
LOG2E = math.log2(math.e)
bf16, f32 = jnp.bfloat16, jnp.float32
LIMIT = 62 * 1024 * 1024
frequency = np.tile(rope_base ** (-np.arange(64) * 2.0 / 128), 2).astype(np.float32)[None]


def dot(a, b, ca, cb):
    return lax.dot_general(a, b, (((ca,), (cb,)), ((), ())), preferred_element_type=f32)


def helpers():
    i = lax.broadcasted_iota(jnp.int32, (128, 128), 0)
    j = lax.broadcasted_iota(jnp.int32, (128, 128), 1)
    swap = ((i == j + 64) | (j == i + 64)).astype(bf16)
    mean = jnp.full((128, 128), 1.0 / 128, bf16)
    return swap, mean


def unit(raw, mean):
    v = raw.astype(f32)
    return lax.rsqrt(dot((v * v).astype(bf16), mean, 1, 0) + norm_eps)


def prepare(raw, gain, cos, sin, swap, mean):
    inv = unit(raw, mean)
    u = raw.astype(f32) * inv * gain
    ru = dot(raw, swap, 1, 0) * inv * pltpu.roll(gain, 64, 1)
    return u * cos + ru * sin, ru * cos - u * sin


def pull(raw, g, rg, gain, cos, sin, mean):
    v = raw.astype(f32)
    inv = unit(raw, mean)
    gw = (g * cos - rg * sin) * gain
    return inv * (gw - v * (inv * inv * dot((gw * v).astype(bf16), mean, 1, 0)))


def turns(start, count, freq):
    positions = (start + lax.broadcasted_iota(jnp.int32, (count, 128), 0)).astype(f32)
    angles = positions * freq
    upper = lax.broadcasted_iota(jnp.int32, (count, 128), 1) >= 64
    sine = jnp.sin(angles)
    return jnp.cos(angles), jnp.where(upper, sine, -sine)


def ready(q_ref, gain_ref, freq_ref, off_ref, second_ref, facts_ref, far_ref, qs_ref, cw_ref, sw_ref, copies_ref, *, heads, plen):
    count = second_ref.shape[0]
    pair = jnp.concatenate([facts_ref[0:1], far_ref[0:1], jnp.zeros((14, 256), bf16)], axis=0)
    for c in range(copies_ref.shape[0]):
        copies_ref[c, :count] = second_ref[...]
        copies_ref[c, count:] = pair

    swap, mean = helpers()
    gain = gain_ref[...] * (LOG2E / math.sqrt(128))
    win = cw_ref.shape[1]
    cw, sw = turns(plen + off_ref[pl.program_id(0)], win, freq_ref[...])
    cw_ref[0] = cw
    sw_ref[0] = sw
    cos, sin = (jnp.concatenate([x] * heads, axis=0) for x in (cw, sw))
    q = jnp.concatenate([q_ref[0, :, g * 128 : (g + 1) * 128] for g in range(heads)], axis=0)
    qs_ref[0] = prepare(q, gain, cos, sin, swap, mean)[0].astype(bf16).reshape(heads, win, 128)


def summary(f):
    reward = [f[:, 3 * n : 3 * n + 1] + f[:, 3 * n + 1 : 3 * n + 2] + f[:, 3 * n + 2 : 3 * n + 3] for n in range(2)]
    place = [f[:, 6 + n : 7 + n] for n in range(2)]
    means = [
        sum(jnp.sum(jnp.where(place[n] == p, reward[n], 0.0), axis=0, keepdims=True) for n in range(2)) / f.shape[0] for p in range(2)
    ]
    spread = sum(jnp.sum((reward[n] - jnp.where(place[n] == 0, means[0], means[1])) ** 2, axis=0, keepdims=True) for n in range(2))
    return means, spread


def attend(
    scalar, qs_ref, q_ref, up_ref, ga_ref, gb_ref, fa_ref, fb_ref, wk_ref, wv_ref, qg_ref, kg_ref, cw_ref, sw_ref, rw_ref, *refs,
    heads, subs, tc, tok, win
):
    att_ref, dq_ref, dwin_ref, stat_ref, *outs = refs[-12:-6]
    kp, va, dk, dv, e_ref, ds_ref = refs[-6:]
    r, hb = pl.program_id(0), pl.program_id(1)
    chips = ga_ref.shape[0]
    half = chips * tok
    plen = 2 * half
    t = plen + win
    root = math.sqrt(128)
    kgain = kg_ref[...]
    swap, mean = helpers()

    @pl.when(hb == 0)
    def _():
        for i, g_ref in enumerate((ga_ref, gb_ref)):
            raw = g_ref[...].reshape(half, 256)
            rows = pl.ds(i * half, half)
            kp[rows, :128] = raw[:, :128]
            kp[rows, 128:] = dot(raw[:, :128], swap, 1, 0).astype(bf16)
            va[rows, :128] = raw[:, 128:]
        k, rk = prepare(wk_ref[0], kgain, cw_ref[0], sw_ref[0], swap, mean)
        kp[plen:, :128] = k.astype(bf16)
        kp[plen:, 128:] = rk.astype(bf16)
        va[plen:, :128] = wv_ref[0]
        va[:, 128:] = jnp.ones_like(va[:, 128:])
        dk[r] = jnp.zeros_like(dk[r])
        dv[r] = jnp.zeros_like(dv[r])

    sh = heads // subs
    rows = sh * win
    i = lax.broadcasted_iota(jnp.int32, (rows, win), 0) % win
    j = lax.broadcasted_iota(jnp.int32, (rows, win), 1)
    seen = i >= j
    S = range(subs)
    chunks = [slice(c, min(c + tc, plen)) for c in range(0, plen, tc)] + [slice(plen, t)]
    block = [slice(b * rows, (b + 1) * rows) for b in S]
    qs = [qs_ref[0, b * sh : (b + 1) * sh].reshape(rows, 128) for b in S]
    for b in S:
        for c in chunks:
            e = jnp.exp2(dot(qs[b], kp[c, :128], 1, 1))
            if c.start == plen:
                e = jnp.where(seen, e, 0.0)
            e_ref[block[b], c] = e.astype(bf16)
    od = [dot(e_ref[block[b]], va[...], 1, 0) for b in S]
    a = []
    for b in S:
        rinv = 1.0 / od[b][:, 128:]
        o = od[b][:, :128] * rinv
        ob = o.astype(bf16)
        up = []
        for g in range(sh):
            cols = slice((b * sh + g) * 128, (b * sh + g + 1) * 128)
            att_ref[0, :, cols] = ob[g * win : (g + 1) * win]
            up.append(up_ref[0, :, cols])
        do = jnp.concatenate(up, axis=0).astype(f32) * rinv
        a.append(jnp.concatenate([do.astype(bf16), (-(do * o)).astype(bf16)], axis=1))
    for b in S:
        for c in chunks:
            ds_ref[block[b], c] = e_ref[block[b], c] * dot(a[b], va[c], 1, 1).astype(bf16)
    gq = [dot(ds_ref[block[b]], kp[...], 1, 0) for b in S]
    cos, sin = (jnp.concatenate([x[0]] * sh, axis=0) for x in (cw_ref, sw_ref))
    for b in S:
        q = jnp.concatenate([q_ref[0, :, (b * sh + g) * 128 : (b * sh + g + 1) * 128] for g in range(sh)], axis=0)
        dq = pull(q, gq[b][:, :128], gq[b][:, 128:], qg_ref[...] * (1.0 / root), cos, sin, mean).astype(bf16)
        for g in range(sh):
            dq_ref[0, :, (b * sh + g) * 128 : (b * sh + g + 1) * 128] = dq[g * win : (g + 1) * win]
    cat = lambda x: jnp.concatenate(x, axis=0) if subs > 1 else x[0]
    dv[r] += dot(cat(a)[:, :128], e_ref[...], 0, 0)
    dk[r] += dot(cat(qs), ds_ref[...], 0, 0)

    @pl.when(hb == pl.num_programs(1) - 1)
    def _():
        ln2 = 1.0 / LOG2E
        gk = dk[r, :, plen:].T * ln2
        dwin_ref[0, :, :128] = pull(wk_ref[0], gk, pltpu.roll(gk, 64, 1), kgain, cw_ref[0], sw_ref[0], mean)
        dwin_ref[0, :, 128:] = dv[r, :, plen:].T

        @pl.when(r == 1)
        def _():
            f = jnp.concatenate([fa_ref[...].reshape(chips, 16, 256), fb_ref[...].reshape(chips, 16, 256)], axis=0).astype(f32)
            means, spread = summary(f[:, 0])
            spread += summary(f[:, 1])[1]
            centred = [rw_ref[n] - jnp.where(scalar[n] == 0, means[0], means[1]) for n in range(2)]
            lane = lax.broadcasted_iota(jnp.int32, stat_ref.shape, 1)
            stat_ref[...] = jnp.where(lane == 0, spread, jnp.where(lane == 1, centred[0], centred[1]))
            for i in range(2):
                cols = pl.ds(i * half, half)
                for p in range(2):
                    for c, (acc, scale) in enumerate(((dk, ln2), (dv, 1.0))):
                        w = [jnp.where(scalar[n] == p, centred[n], 0.0) * scale for n in range(2)]
                        m = (w[0] * acc[0, :, cols] + w[1] * acc[1, :, cols]).astype(bf16).T.reshape(chips, tok, 128)
                        outs[i][:, p * tok : (p + 1) * tok, c * 128 : (c + 1) * 128] = m


def call(h, heads, subs, tc, scalar, qs, q, up, ga, gb, wc, qgain, kgain, cw, sw, rewards, tok, prompts, *before):
    rolls, win, width = up.shape
    chips = ga.shape[0]
    kvh = wc.shape[2] // 256
    share = width // (128 * kvh)
    half = chips * tok
    plen = 2 * half
    steps = share // heads
    t = plen + win
    smem = pl.BlockSpec(memory_space=pltpu.SMEM)
    anywhere = pl.BlockSpec(memory_space=pl.ANY)
    spot = prompts * tok // 16
    if ga.ndim == 3:
        gspecs = [pl.BlockSpec((chips, tok, 256), lambda r, b, a: (0, a[r], 0))] * 2
        gspecs += [pl.BlockSpec((chips, 16, 256), lambda r, b, a: (0, spot, 0))] * 2
    else:
        gspecs = [
            pl.BlockSpec((chips, 1, tok, 256), lambda r, b, a: (0, a[2], a[r], 0)),
            pl.BlockSpec((chips, 1, tok, 256), lambda r, b, a: (0, 1 - a[2], a[r], 0)),
            pl.BlockSpec((chips, 1, 16, 256), lambda r, b, a: (0, a[2], spot, 0)),
            pl.BlockSpec((chips, 1, 16, 256), lambda r, b, a: (0, 1 - a[2], spot, 0)),
        ]
    ospec = pl.BlockSpec((1, win, heads * 128), lambda r, b, a: (r, 0, h * steps + b))
    vec = pl.BlockSpec((1, 128), lambda r, b, a: (0, 0))
    wspec = pl.BlockSpec((1, win, 128), lambda r, b, a: (r, 0, 0))
    piece = (chips, prompts * tok, 256)
    pieces = pl.BlockSpec(piece, lambda r, b, a: (0,) * len(piece))
    return pl.pallas_call(
        functools.partial(attend, heads=heads, subs=subs, tc=tc, tok=tok, win=win),
        grid_spec=pltpu.PrefetchScalarGridSpec(
            num_scalar_prefetch=1,
            grid=(rolls, steps),
            in_specs=[
                pl.BlockSpec((1, heads, win, 128), lambda r, b, a: (r, h * steps + b, 0, 0)),
                ospec,
                ospec,
                *gspecs,
                pl.BlockSpec((1, win, 128), lambda r, b, a: (r, 0, h)),
                pl.BlockSpec((1, win, 128), lambda r, b, a: (r, 0, kvh + h)),
                vec,
                vec,
                wspec,
                wspec,
                smem,
            ]
            + [anywhere] * len(before),
            out_specs=[
                ospec,
                ospec,
                pl.BlockSpec((1, win, 256), lambda r, b, a: (r, 0, 0)),
                pl.BlockSpec((8, 128), lambda r, b, a: (0, 0)),
            ]
            + [pieces] * 2,
            scratch_shapes=[
                pltpu.VMEM((t, 256), bf16),
                pltpu.VMEM((t, 256), bf16),
                pltpu.VMEM((rolls, 128, t), f32),
                pltpu.VMEM((rolls, 128, t), f32),
                pltpu.VMEM((heads * win, t), bf16),
                pltpu.VMEM((heads * win, t), bf16),
            ],
        ),
        out_shape=[
            jax.ShapeDtypeStruct(up.shape, bf16),
            jax.ShapeDtypeStruct(up.shape, bf16),
            jax.ShapeDtypeStruct((rolls, win, 256), f32),
            jax.ShapeDtypeStruct((8, 128), f32),
        ]
        + [jax.ShapeDtypeStruct(piece, bf16)] * 2,
        input_output_aliases={15: 0, 16: 1} if before else {},
        compiler_params=pltpu.CompilerParams(vmem_limit_bytes=LIMIT),
        cost_estimate=pl.CostEstimate(
            flops=36 * rolls * share * win * t * 128, bytes_accessed=10 * rolls * share * win * 128, transcendentals=rolls * share * win * t
        ),
        name="attend",
    )(scalar, qs, q, up, ga, gb, ga, gb, wc, wc, qgain, kgain, cw, sw, rewards, *before)


def make_ready(q, gain, offsets, second, facts, far, plen, members):
    rolls, win, width = q.shape
    heads = width // 128
    wspec = pl.BlockSpec((1, win, 128), lambda r: (r, 0, 0))
    vec = pl.BlockSpec((1, 128), lambda r: (0, 0))
    fspec = pl.BlockSpec((16, 256), lambda r: (0, 0))
    return pl.pallas_call(
        functools.partial(ready, heads=heads, plen=plen),
        grid=(rolls,),
        in_specs=[pl.BlockSpec((1, win, width), lambda r: (r, 0, 0)), vec, vec, pl.BlockSpec(memory_space=pltpu.SMEM), pl.BlockSpec(second.shape, lambda r: (0, 0)), fspec, fspec],
        out_specs=[
            pl.BlockSpec((1, heads, win, 128), lambda r: (r, 0, 0, 0)),
            wspec,
            wspec,
            pl.BlockSpec((members // rolls, second.shape[0] + 16, 256), lambda r: (r, 0, 0)),
        ],
        out_shape=[jax.ShapeDtypeStruct((rolls, heads, win, 128), bf16)]
        + [jax.ShapeDtypeStruct((rolls, win, 128), f32)] * 2
        + [jax.ShapeDtypeStruct((members, second.shape[0] + 16, 256), bf16)],
        compiler_params=pltpu.CompilerParams(vmem_limit_bytes=LIMIT),
        name="ready",
    )(q, gain, frequency, offsets, second, facts, far)


def pack(cache_ref, reward_ref, assign_ref, kg_ref, freq_ref, mine_ref, first_ref, second_ref, facts_ref):
    prompts, tok, width = cache_ref.shape
    kvh = width // 256
    lane = lax.broadcasted_iota(jnp.int32, (16, 256), 1)
    facts = jnp.zeros((16, 256), f32)
    for n in range(2):
        rest = jnp.full((16, 256), reward_ref[n], f32)
        for k in range(3):
            piece = rest.astype(bf16).astype(f32)
            facts = jnp.where(lane == 3 * n + k, piece, facts)
            rest = rest - piece
        facts = jnp.where(lane == 6 + n, assign_ref[n].astype(f32), facts)
    swap, mean = helpers()
    cos, sin = turns(mine_ref[0] * tok, tok, freq_ref[...])
    order = [(p, h) for p in range(prompts) for h in range(kvh)]
    raw = jnp.concatenate([cache_ref[p, :, h * 128 : (h + 1) * 128] for p, h in order], axis=0)
    cos, sin = (jnp.concatenate([x] * len(order), axis=0) for x in (cos, sin))
    keys = prepare(raw, kg_ref[...], cos, sin, swap, mean)[0].astype(bf16)
    for n, (p, h) in enumerate(order):
        key, value = keys[n * tok : (n + 1) * tok], cache_ref[p, :, (kvh + h) * 128 : (kvh + h + 1) * 128]
        if h == 0:
            for c in range(first_ref.shape[0]):
                first_ref[c, p * tok : (p + 1) * tok, :128] = key
                first_ref[c, p * tok : (p + 1) * tok, 128:] = value
        else:
            second_ref[p * tok : (p + 1) * tok, :128] = key
            second_ref[p * tok : (p + 1) * tok, 128:] = value
    facts = jnp.where(lax.broadcasted_iota(jnp.int32, (16, 256), 0) == 0, facts, 0.0).astype(bf16)
    facts_ref[...] = facts
    for c in range(first_ref.shape[0]):
        first_ref[c, prompts * tok :] = facts


def make_pack(cache, rewards, assign, kgain, mine, chips):
    prompts, tok, _ = cache.shape
    smem, vmem = pl.BlockSpec(memory_space=pltpu.SMEM), pl.BlockSpec(memory_space=pltpu.VMEM)
    return pl.pallas_call(
        pack,
        in_specs=[vmem, smem, smem, vmem, vmem, smem],
        out_specs=[vmem, vmem, vmem],
        out_shape=[
            jax.ShapeDtypeStruct((chips, prompts * tok + 16, 256), bf16),
            jax.ShapeDtypeStruct((prompts * tok, 256), bf16),
            jax.ShapeDtypeStruct((16, 256), bf16),
        ],
        name="pack",
    )(cache, rewards, assign, kgain, frequency, mine)


def global_scale(sums_ref, count):
    return 1.0 / jnp.sqrt(sums_ref[0:1, 0:1] / count + spread_eps)


def rescale(dq_ref, dw0_ref, dw1_ref, sums_ref, stat_ref, dq_out, dw_out, *, count):
    r = pl.program_id(0)
    adv = jnp.where(r == 0, stat_ref[0:1, 1:2], stat_ref[0:1, 2:3]) * global_scale(sums_ref, count)
    dq_out[...] = (dq_ref[...].astype(f32) * adv).astype(bf16)
    for n, part in enumerate((dw0_ref, dw1_ref)):
        for c in range(2):
            dw_out[0, :, (2 * c + n) * 128 : (2 * c + n + 1) * 128] = (part[0, :, c * 128 : (c + 1) * 128] * adv).astype(bf16)


def make_rescale(dq, dw0, dw1, sums, stat, count):
    rolls, win, width = dq.shape
    half = pl.BlockSpec((1, win, 256), lambda r: (r, 0, 0))
    qspec = pl.BlockSpec((1, win, width), lambda r: (r, 0, 0))
    return pl.pallas_call(
        functools.partial(rescale, count=count),
        grid=(rolls,),
        in_specs=[
            qspec,
            half,
            half,
            pl.BlockSpec((8, 128), lambda r: (0, 0)),
            pl.BlockSpec((8, 128), lambda r: (0, 0)),
        ],
        out_specs=[qspec, pl.BlockSpec((1, win, 512), lambda r: (r, 0, 0))],
        out_shape=[jax.ShapeDtypeStruct(dq.shape, bf16), jax.ShapeDtypeStruct((rolls, win, 512), bf16)],
        input_output_aliases={0: 0},
        compiler_params=pltpu.CompilerParams(vmem_limit_bytes=LIMIT),
        name="rescale",
    )(dq, dw0, dw1, sums, stat)


def settle(d_ref, cache_ref, kg_ref, freq_ref, mine_ref, sums_ref, out_ref, *, count):
    prompts, tok, width = cache_ref.shape
    scale = global_scale(sums_ref, count)
    _, mean = helpers()
    cos, sin = turns(mine_ref[0] * tok, tok, freq_ref[...])
    for h in range(width // 256):
        for p in range(prompts):
            cut = slice((h * prompts + p) * tok, (h * prompts + p + 1) * tok)
            g = d_ref[0, cut].astype(f32)
            for m in range(1, d_ref.shape[0]):
                g += d_ref[m, cut].astype(f32)
            g *= scale
            key = pull(cache_ref[p, :, h * 128 : (h + 1) * 128], g[:, :128], pltpu.roll(g[:, :128], 64, 1), kg_ref[...], cos, sin, mean)
            out_ref[p, :, h * 128 : (h + 1) * 128] = key.astype(bf16)
            out_ref[p, :, (2 + h) * 128 : (3 + h) * 128] = g[:, 128:].astype(bf16)


def make_settle(d, cache, kgain, mine, sums, count):
    smem, vmem = pl.BlockSpec(memory_space=pltpu.SMEM), pl.BlockSpec(memory_space=pltpu.VMEM)
    return pl.pallas_call(
        functools.partial(settle, count=count),
        grid=(1,),
        in_specs=[vmem, vmem, vmem, vmem, smem, vmem],
        out_specs=vmem,
        out_shape=jax.ShapeDtypeStruct(cache.shape, bf16),
        compiler_params=pltpu.CompilerParams(vmem_limit_bytes=LIMIT),
        name="settle",
    )(d, cache, kgain, frequency, mine, sums)


def local(prompt_cache, key_gain, query_gain, window_cache, queries, upstream, rewards, assign, offsets):
    groups, members = lax.axis_size("prompt"), lax.axis_size("roll")
    rolls = queries.shape[0]
    prompts, tok, _ = prompt_cache.shape
    chips = members // 2
    mine = lax.axis_index("roll")
    same_core = [[2 * c + k for c in range(chips)] for k in range(2)]
    other_core = [(m, m ^ 1) for m in range(members)]

    def flip(x):
        return lax.ppermute(x, "roll", other_core)

    def far(x, step):
        return lax.ppermute(x, "prompt", [(i, i ^ step) for i in range(groups)])

    mine = mine.astype(jnp.int32)[None]
    qgain, kgain = query_gain[None], key_gain[None]
    first, second, facts = make_pack(prompt_cache, rewards, assign, kgain, mine, chips)
    ga = lax.all_to_all(first, "roll", 0, 0, tiled=True, axis_index_groups=same_core)
    scalar = jnp.concatenate([assign, mine % 2])
    qs, cw, sw, copies = make_ready(queries, qgain, offsets, second, facts, far(facts, 1), members * tok, members)
    ga, qs, cw, sw, scalar = lax.optimization_barrier((ga, qs, cw, sw, scalar))
    gb = flip(ga)
    copies, _ = lax.optimization_barrier((copies, ga))
    g1 = lax.all_to_all(copies, "roll", 0, 0, tiled=True).reshape(chips, 2, prompts * tok + 16, 256)

    def attention(h, a, b, *before):
        return call(
            h, 16, 4, 512, scalar, qs, queries, upstream, a, b, window_cache, qgain, kgain, cw, sw, rewards, tok, prompts, *before
        )

    att, dq, dw0, _, own0, other0 = attention(0, ga, gb)
    att, dq, dw1, stat, own1, other1 = attention(1, g1, g1, att, dq)
    merged = [(own.astype(f32) + flip(other).astype(f32)).astype(bf16) for own, other in ((own0, other0), (own1, other1))]
    merged = jnp.concatenate(merged, axis=1)
    parts = lax.all_to_all(merged, "roll", 0, 0, tiled=True, axis_index_groups=same_core)
    sums, step = stat, 2
    while step < groups:
        sums = sums + far(sums, step)
        step *= 2
    count = groups * members * rolls
    dq, window_grad = make_rescale(dq, dw0, dw1, sums, stat, count)
    prompt_grad = make_settle(parts, prompt_cache, kgain, mine, sums, count)
    return att, dq, window_grad, prompt_grad


def solution(mesh):
    both = P(("prompt", "roll"))
    return jax.shard_map(
        local,
        mesh=mesh,
        in_specs=(P("prompt", "roll", None), P(), P(), both, both, both, both, both, both),
        out_specs=(both, both, both, P("prompt", "roll", None)),
        check_vma=False,
    )
```

```python
import functools
import math

import jax
import jax.numpy as jnp
import numpy as np
from jax import lax
from jax.experimental import pallas as pl
from jax.experimental.pallas import tpu as pltpu
from jax.sharding import PartitionSpec as P

rope_base = 1000000.0
norm_eps = 1e-06
spread_eps = 1e-06
LOG2E = math.log2(math.e)
bf16, f32 = jnp.bfloat16, jnp.float32
LIMIT = 63 * 1024 * 1024
frequency = np.tile(rope_base ** (-np.arange(64) * 2.0 / 128), 2).astype(np.float32)[None]


def dot(a, b, ca, cb):
    return lax.dot_general(a, b, (((ca,), (cb,)), ((), ())), preferred_element_type=f32)


def helpers():
    i = lax.broadcasted_iota(jnp.int32, (128, 128), 0)
    j = lax.broadcasted_iota(jnp.int32, (128, 128), 1)
    swap = ((i == j + 64) | (j == i + 64)).astype(bf16)
    mean = jnp.full((128, 128), 1.0 / 128, bf16)
    return swap, mean


def unit(raw, mean):
    v = raw.astype(f32)
    return lax.rsqrt(dot((v * v).astype(bf16), mean, 1, 0) + norm_eps)


def prepare(raw, gain, cos, sin, swap, mean):
    inv = unit(raw, mean)
    u = raw.astype(f32) * inv * gain
    ru = dot(raw, swap, 1, 0) * inv * pltpu.roll(gain, 64, 1)
    return u * cos + ru * sin, ru * cos - u * sin


def pull(raw, g, rg, gain, cos, sin, mean):
    v = raw.astype(f32)
    inv = unit(raw, mean)
    gw = (g * cos - rg * sin) * gain
    return inv * (gw - v * (inv * inv * dot((gw * v).astype(bf16), mean, 1, 0)))


def turns(start, count, freq):
    positions = (start + lax.broadcasted_iota(jnp.int32, (count, 128), 0)).astype(f32)
    angles = positions * freq
    upper = lax.broadcasted_iota(jnp.int32, (count, 128), 1) >= 64
    sine = jnp.sin(angles)
    return jnp.cos(angles), jnp.where(upper, sine, -sine)


def ready(q_ref, gain_ref, freq_ref, off_ref, second_ref, facts_ref, far_ref, qs_ref, cw_ref, sw_ref, copies_ref, *, heads, plen):
    count = second_ref.shape[0]
    pair = jnp.concatenate([facts_ref[0:1], far_ref[0:1], jnp.zeros((14, 256), bf16)], axis=0)
    for c in range(copies_ref.shape[0]):
        copies_ref[c, :count] = second_ref[...]
        copies_ref[c, count:] = pair

    swap, mean = helpers()
    gain = gain_ref[...] * (LOG2E / math.sqrt(128))
    win = cw_ref.shape[1]
    cw, sw = turns(plen + off_ref[pl.program_id(0)], win, freq_ref[...])
    cw_ref[0] = cw
    sw_ref[0] = sw
    cos, sin = (jnp.concatenate([x] * heads, axis=0) for x in (cw, sw))
    q = jnp.concatenate([q_ref[0, :, g * 128 : (g + 1) * 128] for g in range(heads)], axis=0)
    qs_ref[0] = prepare(q, gain, cos, sin, swap, mean)[0].astype(bf16).reshape(heads, win, 128)


def summary(f):
    reward = [f[:, 3 * n : 3 * n + 1] + f[:, 3 * n + 1 : 3 * n + 2] + f[:, 3 * n + 2 : 3 * n + 3] for n in range(2)]
    place = [f[:, 6 + n : 7 + n] for n in range(2)]
    means = [
        sum(jnp.sum(jnp.where(place[n] == p, reward[n], 0.0), axis=0, keepdims=True) for n in range(2)) / f.shape[0] for p in range(2)
    ]
    spread = sum(jnp.sum((reward[n] - jnp.where(place[n] == 0, means[0], means[1])) ** 2, axis=0, keepdims=True) for n in range(2))
    return means, spread


def attend(
    scalar, qs_ref, q_ref, up_ref, ga_ref, gb_ref, fa_ref, fb_ref, wk_ref, wv_ref, qg_ref, kg_ref, cw_ref, sw_ref, rw_ref, *refs,
    heads, subs, tc, tok, win
):
    att_ref, dq_ref, dwin_ref, stat_ref, *outs = refs[-12:-6]
    kp, va, dk, dv, e_ref, ds_ref = refs[-6:]
    r, hb = pl.program_id(0), pl.program_id(1)
    chips = ga_ref.shape[0]
    half = chips * tok
    plen = 2 * half
    t = plen + win
    root = math.sqrt(128)
    kgain = kg_ref[...]
    swap, mean = helpers()

    @pl.when(hb == 0)
    def _():
        for i, g_ref in enumerate((ga_ref, gb_ref)):
            raw = g_ref[...].reshape(half, 256)
            rows = pl.ds(i * half, half)
            kp[rows, :128] = raw[:, :128]
            kp[rows, 128:] = dot(raw[:, :128], swap, 1, 0).astype(bf16)
            va[rows, :128] = raw[:, 128:]
        k, rk = prepare(wk_ref[0], kgain, cw_ref[0], sw_ref[0], swap, mean)
        kp[plen:, :128] = k.astype(bf16)
        kp[plen:, 128:] = rk.astype(bf16)
        va[plen:, :128] = wv_ref[0]
        va[:, 128:] = jnp.ones_like(va[:, 128:])

    sh = heads // subs
    rows = sh * win
    i = lax.broadcasted_iota(jnp.int32, (rows, win), 0) % win
    j = lax.broadcasted_iota(jnp.int32, (rows, win), 1)
    seen = i >= j
    S = range(subs)
    chunks = [slice(c, min(c + tc, plen)) for c in range(0, plen, tc)] + [slice(plen, t)]
    block = [slice(b * rows, (b + 1) * rows) for b in S]
    qs = [qs_ref[0, b * sh : (b + 1) * sh].reshape(rows, 128) for b in S]
    for b in S:
        for c in chunks:
            e = jnp.exp2(dot(qs[b], kp[c, :128], 1, 1))
            if c.start == plen:
                e = jnp.where(seen, e, 0.0)
            e_ref[block[b], c] = e.astype(bf16)
    od = [dot(e_ref[block[b]], va[...], 1, 0) for b in S]
    a = []
    for b in S:
        rinv = 1.0 / od[b][:, 128:]
        o = od[b][:, :128] * rinv
        ob = o.astype(bf16)
        up = []
        for g in range(sh):
            cols = slice((b * sh + g) * 128, (b * sh + g + 1) * 128)
            att_ref[0, :, cols] = ob[g * win : (g + 1) * win]
            up.append(up_ref[0, :, cols])
        do = jnp.concatenate(up, axis=0).astype(f32) * rinv
        a.append(jnp.concatenate([do.astype(bf16), (-(do * o)).astype(bf16)], axis=1))
    for b in S:
        for c in chunks:
            ds_ref[block[b], c] = e_ref[block[b], c] * dot(a[b], va[c], 1, 1).astype(bf16)
    gq = [dot(ds_ref[block[b]], kp[...], 1, 0) for b in S]
    cos, sin = (jnp.concatenate([x[0]] * sh, axis=0) for x in (cw_ref, sw_ref))
    for b in S:
        q = jnp.concatenate([q_ref[0, :, (b * sh + g) * 128 : (b * sh + g + 1) * 128] for g in range(sh)], axis=0)
        dq = pull(q, gq[b][:, :128], gq[b][:, 128:], qg_ref[...] * (1.0 / root), cos, sin, mean).astype(bf16)
        for g in range(sh):
            dq_ref[0, :, (b * sh + g) * 128 : (b * sh + g + 1) * 128] = dq[g * win : (g + 1) * win]
    cat = lambda x: jnp.concatenate(x, axis=0) if subs > 1 else x[0]
    dv[r] = dot(cat(a)[:, :128], e_ref[...], 0, 0)
    dk[r] = dot(cat(qs), ds_ref[...], 0, 0)

    @pl.when(hb == pl.num_programs(1) - 1)
    def _():
        ln2 = 1.0 / LOG2E
        gk = dk[r, :, plen:].T * ln2
        dwin_ref[0, :, :128] = pull(wk_ref[0], gk, pltpu.roll(gk, 64, 1), kgain, cw_ref[0], sw_ref[0], mean)
        dwin_ref[0, :, 128:] = dv[r, :, plen:].T

        @pl.when(r == 1)
        def _():
            f = jnp.concatenate([fa_ref[...].reshape(chips, 16, 256), fb_ref[...].reshape(chips, 16, 256)], axis=0).astype(f32)
            means, spread = summary(f[:, 0])
            spread += summary(f[:, 1])[1]
            centred = [rw_ref[n] - jnp.where(scalar[n] == 0, means[0], means[1]) for n in range(2)]
            lane = lax.broadcasted_iota(jnp.int32, stat_ref.shape, 1)
            stat_ref[...] = jnp.where(lane == 0, spread, jnp.where(lane == 1, centred[0], centred[1]))
            for i in range(2):
                cols = pl.ds(i * half, half)
                for p in range(2):
                    for c, (acc, scale) in enumerate(((dk, ln2), (dv, 1.0))):
                        w = [jnp.where(scalar[n] == p, centred[n], 0.0) * scale for n in range(2)]
                        m = (w[0] * acc[0, :, cols] + w[1] * acc[1, :, cols]).astype(bf16).T.reshape(chips, tok, 128)
                        outs[i][:, p * tok : (p + 1) * tok, c * 128 : (c + 1) * 128] = m


def call(h, subs, tc, scalar, qs, q, up, ga, gb, wc, qgain, kgain, cw, sw, rewards, tok, prompts, *before):
    rolls, win, width = up.shape
    chips = ga.shape[0]
    kvh = wc.shape[2] // 256
    share = width // (128 * kvh)
    half = chips * tok
    plen = 2 * half
    heads, steps = share, 1
    t = plen + win
    smem = pl.BlockSpec(memory_space=pltpu.SMEM)
    anywhere = pl.BlockSpec(memory_space=pl.ANY)
    spot = prompts * tok // 16
    if ga.ndim == 3:
        gspecs = [pl.BlockSpec((chips, tok, 256), lambda r, b, a: (0, a[r], 0))] * 2
        gspecs += [pl.BlockSpec((chips, 16, 256), lambda r, b, a: (0, spot, 0))] * 2
    else:
        gspecs = [
            pl.BlockSpec((chips, 1, tok, 256), lambda r, b, a: (0, a[2], a[r], 0)),
            pl.BlockSpec((chips, 1, tok, 256), lambda r, b, a: (0, 1 - a[2], a[r], 0)),
            pl.BlockSpec((chips, 1, 16, 256), lambda r, b, a: (0, a[2], spot, 0)),
            pl.BlockSpec((chips, 1, 16, 256), lambda r, b, a: (0, 1 - a[2], spot, 0)),
        ]
    ospec = pl.BlockSpec((1, win, heads * 128), lambda r, b, a: (r, 0, h * steps + b))
    vec = pl.BlockSpec((1, 128), lambda r, b, a: (0, 0))
    wspec = pl.BlockSpec((1, win, 128), lambda r, b, a: (r, 0, 0))
    piece = (chips, prompts * tok, 256)
    pieces = pl.BlockSpec(piece, lambda r, b, a: (0,) * len(piece))
    return pl.pallas_call(
        functools.partial(attend, heads=heads, subs=subs, tc=tc, tok=tok, win=win),
        grid_spec=pltpu.PrefetchScalarGridSpec(
            num_scalar_prefetch=1,
            grid=(rolls, steps),
            in_specs=[
                pl.BlockSpec((1, heads, win, 128), lambda r, b, a: (r, h * steps + b, 0, 0)),
                ospec,
                ospec,
                *gspecs,
                pl.BlockSpec((1, win, 128), lambda r, b, a: (r, 0, h)),
                pl.BlockSpec((1, win, 128), lambda r, b, a: (r, 0, kvh + h)),
                vec,
                vec,
                wspec,
                wspec,
                smem,
            ]
            + [anywhere] * len(before),
            out_specs=[
                ospec,
                ospec,
                pl.BlockSpec((1, win, 256), lambda r, b, a: (r, 0, 0)),
                pl.BlockSpec((8, 128), lambda r, b, a: (0, 0)),
            ]
            + [pieces] * 2,
            scratch_shapes=[
                pltpu.VMEM((t, 256), bf16),
                pltpu.VMEM((t, 256), bf16),
                pltpu.VMEM((rolls, 128, t), f32),
                pltpu.VMEM((rolls, 128, t), f32),
                pltpu.VMEM((heads * win, t), bf16),
                pltpu.VMEM((heads * win, t), bf16),
            ],
        ),
        out_shape=[
            jax.ShapeDtypeStruct(up.shape, bf16),
            jax.ShapeDtypeStruct(up.shape, bf16),
            jax.ShapeDtypeStruct((rolls, win, 256), f32),
            jax.ShapeDtypeStruct((8, 128), f32),
        ]
        + [jax.ShapeDtypeStruct(piece, bf16)] * 2,
        input_output_aliases={15: 0, 16: 1} if before else {},
        compiler_params=pltpu.CompilerParams(vmem_limit_bytes=LIMIT),
        cost_estimate=pl.CostEstimate(
            flops=36 * rolls * share * win * t * 128, bytes_accessed=10 * rolls * share * win * 128, transcendentals=rolls * share * win * t
        ),
        name="attend",
    )(scalar, qs, q, up, ga, gb, ga, gb, wc, wc, qgain, kgain, cw, sw, rewards, *before)


def make_ready(q, gain, offsets, second, facts, far, plen, members):
    rolls, win, width = q.shape
    heads = width // 128
    wspec = pl.BlockSpec((1, win, 128), lambda r: (r, 0, 0))
    vec = pl.BlockSpec((1, 128), lambda r: (0, 0))
    fspec = pl.BlockSpec((16, 256), lambda r: (0, 0))
    return pl.pallas_call(
        functools.partial(ready, heads=heads, plen=plen),
        grid=(rolls,),
        in_specs=[pl.BlockSpec((1, win, width), lambda r: (r, 0, 0)), vec, vec, pl.BlockSpec(memory_space=pltpu.SMEM), pl.BlockSpec(second.shape, lambda r: (0, 0)), fspec, fspec],
        out_specs=[
            pl.BlockSpec((1, heads, win, 128), lambda r: (r, 0, 0, 0)),
            wspec,
            wspec,
            pl.BlockSpec((members // rolls, second.shape[0] + 16, 256), lambda r: (r, 0, 0)),
        ],
        out_shape=[jax.ShapeDtypeStruct((rolls, heads, win, 128), bf16)]
        + [jax.ShapeDtypeStruct((rolls, win, 128), f32)] * 2
        + [jax.ShapeDtypeStruct((members, second.shape[0] + 16, 256), bf16)],
        compiler_params=pltpu.CompilerParams(vmem_limit_bytes=LIMIT - 3 * 1024 * 1024),
        name="ready",
    )(q, gain, frequency, offsets, second, facts, far)


def pack(cache_ref, reward_ref, assign_ref, kg_ref, freq_ref, mine_ref, first_ref, second_ref, facts_ref):
    prompts, tok, width = cache_ref.shape
    kvh = width // 256
    lane = lax.broadcasted_iota(jnp.int32, (16, 256), 1)
    facts = jnp.zeros((16, 256), f32)
    for n in range(2):
        rest = jnp.full((16, 256), reward_ref[n], f32)
        for k in range(3):
            piece = rest.astype(bf16).astype(f32)
            facts = jnp.where(lane == 3 * n + k, piece, facts)
            rest = rest - piece
        facts = jnp.where(lane == 6 + n, assign_ref[n].astype(f32), facts)
    swap, mean = helpers()
    cos, sin = turns(mine_ref[0] * tok, tok, freq_ref[...])
    order = [(p, h) for p in range(prompts) for h in range(kvh)]
    raw = jnp.concatenate([cache_ref[p, :, h * 128 : (h + 1) * 128] for p, h in order], axis=0)
    cos, sin = (jnp.concatenate([x] * len(order), axis=0) for x in (cos, sin))
    keys = prepare(raw, kg_ref[...], cos, sin, swap, mean)[0].astype(bf16)
    for n, (p, h) in enumerate(order):
        key, value = keys[n * tok : (n + 1) * tok], cache_ref[p, :, (kvh + h) * 128 : (kvh + h + 1) * 128]
        if h == 0:
            for c in range(first_ref.shape[0]):
                first_ref[c, p * tok : (p + 1) * tok, :128] = key
                first_ref[c, p * tok : (p + 1) * tok, 128:] = value
        else:
            second_ref[p * tok : (p + 1) * tok, :128] = key
            second_ref[p * tok : (p + 1) * tok, 128:] = value
    facts = jnp.where(lax.broadcasted_iota(jnp.int32, (16, 256), 0) == 0, facts, 0.0).astype(bf16)
    facts_ref[...] = facts
    for c in range(first_ref.shape[0]):
        first_ref[c, prompts * tok :] = facts


def make_pack(cache, rewards, assign, kgain, mine, chips):
    prompts, tok, _ = cache.shape
    smem, vmem = pl.BlockSpec(memory_space=pltpu.SMEM), pl.BlockSpec(memory_space=pltpu.VMEM)
    return pl.pallas_call(
        pack,
        in_specs=[vmem, smem, smem, vmem, vmem, smem],
        out_specs=[vmem, vmem, vmem],
        out_shape=[
            jax.ShapeDtypeStruct((chips, prompts * tok + 16, 256), bf16),
            jax.ShapeDtypeStruct((prompts * tok, 256), bf16),
            jax.ShapeDtypeStruct((16, 256), bf16),
        ],
        name="pack",
    )(cache, rewards, assign, kgain, frequency, mine)


def global_scale(sums_ref, count):
    return 1.0 / jnp.sqrt(sums_ref[0:1, 0:1] / count + spread_eps)


def rescale(dq_ref, dw0_ref, dw1_ref, sums_ref, stat_ref, dq_out, dw_out, *, count):
    r = pl.program_id(0)
    adv = jnp.where(r == 0, stat_ref[0:1, 1:2], stat_ref[0:1, 2:3]) * global_scale(sums_ref, count)
    dq_out[...] = (dq_ref[...].astype(f32) * adv).astype(bf16)
    for n, part in enumerate((dw0_ref, dw1_ref)):
        for c in range(2):
            dw_out[0, :, (2 * c + n) * 128 : (2 * c + n + 1) * 128] = (part[0, :, c * 128 : (c + 1) * 128] * adv).astype(bf16)


def make_rescale(dq, dw0, dw1, sums, stat, count):
    rolls, win, width = dq.shape
    half = pl.BlockSpec((1, win, 256), lambda r: (r, 0, 0))
    qspec = pl.BlockSpec((1, win, width), lambda r: (r, 0, 0))
    return pl.pallas_call(
        functools.partial(rescale, count=count),
        grid=(rolls,),
        in_specs=[
            qspec,
            half,
            half,
            pl.BlockSpec((8, 128), lambda r: (0, 0)),
            pl.BlockSpec((8, 128), lambda r: (0, 0)),
        ],
        out_specs=[qspec, pl.BlockSpec((1, win, 512), lambda r: (r, 0, 0))],
        out_shape=[jax.ShapeDtypeStruct(dq.shape, bf16), jax.ShapeDtypeStruct((rolls, win, 512), bf16)],
        input_output_aliases={0: 0},
        compiler_params=pltpu.CompilerParams(vmem_limit_bytes=LIMIT - 3 * 1024 * 1024),
        name="rescale",
    )(dq, dw0, dw1, sums, stat)


def merge(own0, far0, own1, far1, stat_ref, there_ref, out_ref, sums_ref):
    rows = own0.shape[1]
    for h, (own, far) in enumerate(((own0, far0), (own1, far1))):
        out_ref[:, h * rows : (h + 1) * rows] = (own[...].astype(f32) + far[...].astype(f32)).astype(bf16)
    sums_ref[...] = stat_ref[...] + there_ref[...]


def make_merge(own0, far0, own1, far1, stat, there):
    chips, rows, width = own0.shape
    vmem = pl.BlockSpec(memory_space=pltpu.VMEM)
    return pl.pallas_call(
        merge,
        in_specs=[vmem] * 6,
        out_specs=[vmem, vmem],
        out_shape=[jax.ShapeDtypeStruct((chips, 2 * rows, width), bf16), jax.ShapeDtypeStruct(stat.shape, f32)],
        compiler_params=pltpu.CompilerParams(vmem_limit_bytes=16 * 1024 * 1024),
        name="merge",
    )(own0, far0, own1, far1, stat, there)


def settle(d_ref, cache_ref, kg_ref, freq_ref, mine_ref, sums_ref, out_ref, *, count):
    prompts, tok, width = cache_ref.shape
    scale = global_scale(sums_ref, count)
    _, mean = helpers()
    cos, sin = turns(mine_ref[0] * tok, tok, freq_ref[...])
    for h in range(width // 256):
        for p in range(prompts):
            cut = slice((h * prompts + p) * tok, (h * prompts + p + 1) * tok)
            g = d_ref[0, cut].astype(f32)
            for m in range(1, d_ref.shape[0]):
                g += d_ref[m, cut].astype(f32)
            g *= scale
            key = pull(cache_ref[p, :, h * 128 : (h + 1) * 128], g[:, :128], pltpu.roll(g[:, :128], 64, 1), kg_ref[...], cos, sin, mean)
            out_ref[p, :, h * 128 : (h + 1) * 128] = key.astype(bf16)
            out_ref[p, :, (2 + h) * 128 : (3 + h) * 128] = g[:, 128:].astype(bf16)


def make_settle(d, cache, kgain, mine, sums, count):
    smem, vmem = pl.BlockSpec(memory_space=pltpu.SMEM), pl.BlockSpec(memory_space=pltpu.VMEM)
    return pl.pallas_call(
        functools.partial(settle, count=count),
        grid=(1,),
        in_specs=[vmem, vmem, vmem, vmem, smem, vmem],
        out_specs=vmem,
        out_shape=jax.ShapeDtypeStruct(cache.shape, bf16),
        compiler_params=pltpu.CompilerParams(vmem_limit_bytes=16 * 1024 * 1024),
        name="settle",
    )(d, cache, kgain, frequency, mine, sums)


def local(prompt_cache, key_gain, query_gain, window_cache, queries, upstream, rewards, assign, offsets):
    groups, members = lax.axis_size("prompt"), lax.axis_size("roll")
    rolls = queries.shape[0]
    prompts, tok, _ = prompt_cache.shape
    chips = members // 2
    mine = lax.axis_index("roll")
    same_core = [[2 * c + k for c in range(chips)] for k in range(2)]
    other_core = [(m, m ^ 1) for m in range(members)]

    def flip(x):
        return lax.ppermute(x, "roll", other_core)

    def far(x, step):
        return lax.ppermute(x, "prompt", [(i, i ^ step) for i in range(groups)])

    mine = mine.astype(jnp.int32)[None]
    qgain, kgain = query_gain[None], key_gain[None]
    first, second, facts = make_pack(prompt_cache, rewards, assign, kgain, mine, chips)
    ga = lax.all_to_all(first, "roll", 0, 0, tiled=True, axis_index_groups=same_core)
    scalar = jnp.concatenate([assign, mine % 2])
    qs, cw, sw, copies = make_ready(queries, qgain, offsets, second, facts, far(facts, 1), members * tok, members)
    ga, qs, cw, sw, scalar = lax.optimization_barrier((ga, qs, cw, sw, scalar))
    gb = flip(ga)
    copies, _ = lax.optimization_barrier((copies, ga))
    g1 = lax.all_to_all(copies, "roll", 0, 0, tiled=True).reshape(chips, 2, prompts * tok + 16, 256)

    def attention(h, a, b, *before):
        return call(
            h, 4, 512, scalar, qs, queries, upstream, a, b, window_cache, qgain, kgain, cw, sw, rewards, tok, prompts, *before
        )

    att, dq, dw0, _, own0, other0 = attention(0, ga, gb)
    att, dq, dw1, stat, own1, other1 = attention(1, g1, g1, att, dq)
    merged, sums = make_merge(own0, flip(other0), own1, flip(other1), stat, far(stat, groups // 2))
    parts = lax.all_to_all(merged, "roll", 0, 0, tiled=True, axis_index_groups=same_core)
    step = 2
    while step < groups // 2:
        sums = sums + far(sums, step)
        step *= 2
    count = groups * members * rolls
    dq, window_grad = make_rescale(dq, dw0, dw1, sums, stat, count)
    prompt_grad = make_settle(parts, prompt_cache, kgain, mine, sums, count)
    return att, dq, window_grad, prompt_grad


def solution(mesh):
    both = P(("prompt", "roll"))
    return jax.shard_map(
        local,
        mesh=mesh,
        in_specs=(P("prompt", "roll", None), P(), P(), both, both, both, both, both, both),
        out_specs=(both, both, both, P("prompt", "roll", None)),
        check_vma=False,
    )
```

```python
import functools
import math

import jax
import jax.numpy as jnp
import numpy as np
from jax import lax
from jax.experimental import pallas as pl
from jax.experimental.pallas import tpu as pltpu
from jax.sharding import PartitionSpec as P

rope_base = 1000000.0
norm_eps = 1e-06
spread_eps = 1e-06
LOG2E = math.log2(math.e)
bf16, f32 = jnp.bfloat16, jnp.float32
LIMIT = 63 * 1024 * 1024
frequency = np.tile(rope_base ** (-np.arange(64) * 2.0 / 128), 2).astype(np.float32)[None]


def dot(a, b, ca, cb):
    return lax.dot_general(a, b, (((ca,), (cb,)), ((), ())), preferred_element_type=f32)


def helpers():
    i = lax.broadcasted_iota(jnp.int32, (128, 128), 0)
    j = lax.broadcasted_iota(jnp.int32, (128, 128), 1)
    swap = ((i == j + 64) | (j == i + 64)).astype(bf16)
    mean = jnp.full((128, 128), 1.0 / 128, bf16)
    return swap, mean


def unit(raw, mean):
    v = raw.astype(f32)
    return lax.rsqrt(dot((v * v).astype(bf16), mean, 1, 0) + norm_eps)


def prepare(raw, gain, cos, sin, swap, mean):
    inv = unit(raw, mean)
    u = raw.astype(f32) * inv * gain
    ru = dot(raw, swap, 1, 0) * inv * pltpu.roll(gain, 64, 1)
    return u * cos + ru * sin, ru * cos - u * sin


def pull(raw, g, rg, gain, cos, sin, mean):
    v = raw.astype(f32)
    inv = unit(raw, mean)
    gw = (g * cos - rg * sin) * gain
    return inv * (gw - v * (inv * inv * dot((gw * v).astype(bf16), mean, 1, 0)))


def turns(start, count, freq):
    positions = (start + lax.broadcasted_iota(jnp.int32, (count, 128), 0)).astype(f32)
    angles = positions * freq
    upper = lax.broadcasted_iota(jnp.int32, (count, 128), 1) >= 64
    sine = jnp.sin(angles)
    return jnp.cos(angles), jnp.where(upper, sine, -sine)


def ready(q_ref, gain_ref, freq_ref, off_ref, second_ref, facts_ref, far_ref, qs_ref, cw_ref, sw_ref, copies_ref, *, heads, plen):
    count = second_ref.shape[0]
    pair = jnp.concatenate([facts_ref[0:1], far_ref[0:1], jnp.zeros((14, 256), bf16)], axis=0)
    for c in range(copies_ref.shape[0]):
        copies_ref[c, :count] = second_ref[...]
        copies_ref[c, count:] = pair

    swap, mean = helpers()
    gain = gain_ref[...] * (LOG2E / math.sqrt(128))
    win = cw_ref.shape[1]
    cw, sw = turns(plen + off_ref[pl.program_id(0)], win, freq_ref[...])
    cw_ref[0] = cw
    sw_ref[0] = sw
    cos, sin = (jnp.concatenate([x] * heads, axis=0) for x in (cw, sw))
    q = jnp.concatenate([q_ref[0, :, g * 128 : (g + 1) * 128] for g in range(heads)], axis=0)
    qs_ref[0] = prepare(q, gain, cos, sin, swap, mean)[0].astype(bf16).reshape(heads, win, 128)


def summary(f):
    reward = [f[:, 3 * n : 3 * n + 1] + f[:, 3 * n + 1 : 3 * n + 2] + f[:, 3 * n + 2 : 3 * n + 3] for n in range(2)]
    place = [f[:, 6 + n : 7 + n] for n in range(2)]
    means = [
        sum(jnp.sum(jnp.where(place[n] == p, reward[n], 0.0), axis=0, keepdims=True) for n in range(2)) / f.shape[0] for p in range(2)
    ]
    spread = sum(jnp.sum((reward[n] - jnp.where(place[n] == 0, means[0], means[1])) ** 2, axis=0, keepdims=True) for n in range(2))
    return means, spread


def attend(
    scalar, qs_ref, q_ref, up_ref, ga_ref, gb_ref, fa_ref, fb_ref, wk_ref, wv_ref, qg_ref, kg_ref, cw_ref, sw_ref, rw_ref, *refs,
    heads, subs, tc, tok, win
):
    att_ref, dq_ref, dwin_ref, stat_ref, *outs = refs[-12:-6]
    kp, va, dk, dv, e_ref, ds_ref = refs[-6:]
    r, hb = pl.program_id(0), pl.program_id(1)
    chips = ga_ref.shape[0]
    half = chips * tok
    plen = 2 * half
    t = plen + win
    root = math.sqrt(128)
    kgain = kg_ref[...]
    swap, mean = helpers()

    @pl.when(hb == 0)
    def _():
        for i, g_ref in enumerate((ga_ref, gb_ref)):
            raw = g_ref[...].reshape(half, 256)
            rows = pl.ds(i * half, half)
            kp[rows, :128] = raw[:, :128]
            kp[rows, 128:] = dot(raw[:, :128], swap, 1, 0).astype(bf16)
            va[rows, :128] = raw[:, 128:]
        k, rk = prepare(wk_ref[0], kgain, cw_ref[0], sw_ref[0], swap, mean)
        kp[plen:, :128] = k.astype(bf16)
        kp[plen:, 128:] = rk.astype(bf16)
        va[plen:, :128] = wv_ref[0]
        va[:, 128:] = jnp.ones_like(va[:, 128:])

    sh = heads // subs
    rows = sh * win
    i = lax.broadcasted_iota(jnp.int32, (rows, win), 0) % win
    j = lax.broadcasted_iota(jnp.int32, (rows, win), 1)
    seen = i >= j
    S = range(subs)
    chunks = [slice(c, min(c + tc, plen)) for c in range(0, plen, tc)] + [slice(plen, t)]
    block = [slice(b * rows, (b + 1) * rows) for b in S]
    qs = [qs_ref[0, b * sh : (b + 1) * sh].reshape(rows, 128) for b in S]
    for b in S:
        for c in chunks:
            e = jnp.exp2(dot(qs[b], kp[c, :128], 1, 1))
            if c.start == plen:
                e = jnp.where(seen, e, 0.0)
            e_ref[block[b], c] = e.astype(bf16)
    od = [dot(e_ref[block[b]], va[...], 1, 0) for b in S]
    a = []
    for b in S:
        rinv = 1.0 / od[b][:, 128:]
        o = od[b][:, :128] * rinv
        ob = o.astype(bf16)
        up = []
        for g in range(sh):
            cols = slice((b * sh + g) * 128, (b * sh + g + 1) * 128)
            att_ref[0, :, cols] = ob[g * win : (g + 1) * win]
            up.append(up_ref[0, :, cols])
        do = jnp.concatenate(up, axis=0).astype(f32) * rinv
        a.append(jnp.concatenate([do.astype(bf16), (-(do * o)).astype(bf16)], axis=1))
    for b in S:
        for c in chunks:
            ds_ref[block[b], c] = e_ref[block[b], c] * dot(a[b], va[c], 1, 1).astype(bf16)
    gq = [dot(ds_ref[block[b]], kp[...], 1, 0) for b in S]
    cos, sin = (jnp.concatenate([x[0]] * sh, axis=0) for x in (cw_ref, sw_ref))
    for b in S:
        q = jnp.concatenate([q_ref[0, :, (b * sh + g) * 128 : (b * sh + g + 1) * 128] for g in range(sh)], axis=0)
        dq = pull(q, gq[b][:, :128], gq[b][:, 128:], qg_ref[...] * (1.0 / root), cos, sin, mean).astype(bf16)
        for g in range(sh):
            dq_ref[0, :, (b * sh + g) * 128 : (b * sh + g + 1) * 128] = dq[g * win : (g + 1) * win]
    cat = lambda x: jnp.concatenate(x, axis=0) if subs > 1 else x[0]
    dv[r] = dot(cat(a)[:, :128], e_ref[...], 0, 0)
    dk[r] = dot(cat(qs), ds_ref[...], 0, 0)

    @pl.when(hb == pl.num_programs(1) - 1)
    def _():
        ln2 = 1.0 / LOG2E
        gk = dk[r, :, plen:].T * ln2
        dwin_ref[0, :, :128] = pull(wk_ref[0], gk, pltpu.roll(gk, 64, 1), kgain, cw_ref[0], sw_ref[0], mean)
        dwin_ref[0, :, 128:] = dv[r, :, plen:].T

        @pl.when(r == 1)
        def _():
            f = jnp.concatenate([fa_ref[...].reshape(chips, 16, 256), fb_ref[...].reshape(chips, 16, 256)], axis=0).astype(f32)
            means, spread = summary(f[:, 0])
            spread += summary(f[:, 1])[1]
            centred = [rw_ref[n] - jnp.where(scalar[n] == 0, means[0], means[1]) for n in range(2)]
            lane = lax.broadcasted_iota(jnp.int32, stat_ref.shape, 1)
            stat_ref[...] = jnp.where(lane == 0, spread, jnp.where(lane == 1, centred[0], centred[1]))
            for i in range(2):
                cols = pl.ds(i * half, half)
                for p in range(2):
                    for c, (acc, scale) in enumerate(((dk, ln2), (dv, 1.0))):
                        w = [jnp.where(scalar[n] == p, centred[n], 0.0) * scale for n in range(2)]
                        m = (w[0] * acc[0, :, cols] + w[1] * acc[1, :, cols]).astype(bf16).T.reshape(chips, tok, 128)
                        outs[i][:, p * tok : (p + 1) * tok, c * 128 : (c + 1) * 128] = m


def call(h, subs, tc, scalar, qs, q, up, ga, gb, wc, qgain, kgain, cw, sw, rewards, tok, prompts, *before):
    rolls, win, width = up.shape
    chips = ga.shape[0]
    kvh = wc.shape[2] // 256
    share = width // (128 * kvh)
    half = chips * tok
    plen = 2 * half
    heads, steps = share, 1
    t = plen + win
    smem = pl.BlockSpec(memory_space=pltpu.SMEM)
    anywhere = pl.BlockSpec(memory_space=pl.ANY)
    spot = prompts * tok // 16
    if ga.ndim == 3:
        gspecs = [pl.BlockSpec((chips, tok, 256), lambda r, b, a: (0, a[r], 0))] * 2
        gspecs += [pl.BlockSpec((chips, 16, 256), lambda r, b, a: (0, spot, 0))] * 2
    else:
        gspecs = [
            pl.BlockSpec((chips, 1, tok, 256), lambda r, b, a: (0, a[2], a[r], 0)),
            pl.BlockSpec((chips, 1, tok, 256), lambda r, b, a: (0, 1 - a[2], a[r], 0)),
            pl.BlockSpec((chips, 1, 16, 256), lambda r, b, a: (0, a[2], spot, 0)),
            pl.BlockSpec((chips, 1, 16, 256), lambda r, b, a: (0, 1 - a[2], spot, 0)),
        ]
    ospec = pl.BlockSpec((1, win, heads * 128), lambda r, b, a: (r, 0, h * steps + b))
    vec = pl.BlockSpec((1, 128), lambda r, b, a: (0, 0))
    wspec = pl.BlockSpec((1, win, 128), lambda r, b, a: (r, 0, 0))
    piece = (chips, prompts * tok, 256)
    pieces = pl.BlockSpec(piece, lambda r, b, a: (0,) * len(piece))
    return pl.pallas_call(
        functools.partial(attend, heads=heads, subs=subs, tc=tc, tok=tok, win=win),
        grid_spec=pltpu.PrefetchScalarGridSpec(
            num_scalar_prefetch=1,
            grid=(rolls, steps),
            in_specs=[
                pl.BlockSpec((1, heads, win, 128), lambda r, b, a: (r, h * steps + b, 0, 0)),
                ospec,
                ospec,
                *gspecs,
                pl.BlockSpec((1, win, 128), lambda r, b, a: (r, 0, h)),
                pl.BlockSpec((1, win, 128), lambda r, b, a: (r, 0, kvh + h)),
                vec,
                vec,
                wspec,
                wspec,
                smem,
            ]
            + [anywhere] * len(before),
            out_specs=[
                ospec,
                ospec,
                pl.BlockSpec((1, win, 256), lambda r, b, a: (r, 0, 0)),
                pl.BlockSpec((8, 128), lambda r, b, a: (0, 0)),
            ]
            + [pieces] * 2,
            scratch_shapes=[
                pltpu.VMEM((t, 256), bf16),
                pltpu.VMEM((t, 256), bf16),
                pltpu.VMEM((rolls, 128, t), f32),
                pltpu.VMEM((rolls, 128, t), f32),
                pltpu.VMEM((heads * win, t), bf16),
                pltpu.VMEM((heads * win, t), bf16),
            ],
        ),
        out_shape=[
            jax.ShapeDtypeStruct(up.shape, bf16),
            jax.ShapeDtypeStruct(up.shape, bf16),
            jax.ShapeDtypeStruct((rolls, win, 256), f32),
            jax.ShapeDtypeStruct((8, 128), f32),
        ]
        + [jax.ShapeDtypeStruct(piece, bf16)] * 2,
        input_output_aliases={15: 0, 16: 1} if before else {},
        compiler_params=pltpu.CompilerParams(vmem_limit_bytes=LIMIT),
        cost_estimate=pl.CostEstimate(
            flops=36 * rolls * share * win * t * 128, bytes_accessed=10 * rolls * share * win * 128, transcendentals=rolls * share * win * t
        ),
        name="attend",
    )(scalar, qs, q, up, ga, gb, ga, gb, wc, wc, qgain, kgain, cw, sw, rewards, *before)


def make_ready(q, gain, offsets, second, facts, far, plen, members):
    rolls, win, width = q.shape
    heads = width // 128
    wspec = pl.BlockSpec((1, win, 128), lambda r: (r, 0, 0))
    vec = pl.BlockSpec((1, 128), lambda r: (0, 0))
    fspec = pl.BlockSpec((16, 256), lambda r: (0, 0))
    return pl.pallas_call(
        functools.partial(ready, heads=heads, plen=plen),
        grid=(rolls,),
        in_specs=[pl.BlockSpec((1, win, width), lambda r: (r, 0, 0)), vec, vec, pl.BlockSpec(memory_space=pltpu.SMEM), pl.BlockSpec(second.shape, lambda r: (0, 0)), fspec, fspec],
        out_specs=[
            pl.BlockSpec((1, heads, win, 128), lambda r: (r, 0, 0, 0)),
            wspec,
            wspec,
            pl.BlockSpec((members // rolls, second.shape[0] + 16, 256), lambda r: (r, 0, 0)),
        ],
        out_shape=[jax.ShapeDtypeStruct((rolls, heads, win, 128), bf16)]
        + [jax.ShapeDtypeStruct((rolls, win, 128), f32)] * 2
        + [jax.ShapeDtypeStruct((members, second.shape[0] + 16, 256), bf16)],
        compiler_params=pltpu.CompilerParams(vmem_limit_bytes=LIMIT - 3 * 1024 * 1024),
        name="ready",
    )(q, gain, frequency, offsets, second, facts, far)


def pack(cache_ref, reward_ref, assign_ref, kg_ref, freq_ref, mine_ref, first_ref, second_ref, facts_ref):
    prompts, tok, width = cache_ref.shape
    kvh = width // 256
    lane = lax.broadcasted_iota(jnp.int32, (16, 256), 1)
    facts = jnp.zeros((16, 256), f32)
    for n in range(2):
        rest = jnp.full((16, 256), reward_ref[n], f32)
        for k in range(3):
            piece = rest.astype(bf16).astype(f32)
            facts = jnp.where(lane == 3 * n + k, piece, facts)
            rest = rest - piece
        facts = jnp.where(lane == 6 + n, assign_ref[n].astype(f32), facts)
    swap, mean = helpers()
    cos, sin = turns(mine_ref[0] * tok, tok, freq_ref[...])
    order = [(p, h) for p in range(prompts) for h in range(kvh)]
    raw = jnp.concatenate([cache_ref[p, :, h * 128 : (h + 1) * 128] for p, h in order], axis=0)
    cos, sin = (jnp.concatenate([x] * len(order), axis=0) for x in (cos, sin))
    keys = prepare(raw, kg_ref[...], cos, sin, swap, mean)[0].astype(bf16)
    for n, (p, h) in enumerate(order):
        key, value = keys[n * tok : (n + 1) * tok], cache_ref[p, :, (kvh + h) * 128 : (kvh + h + 1) * 128]
        if h == 0:
            for c in range(first_ref.shape[0]):
                first_ref[c, p * tok : (p + 1) * tok, :128] = key
                first_ref[c, p * tok : (p + 1) * tok, 128:] = value
        else:
            second_ref[p * tok : (p + 1) * tok, :128] = key
            second_ref[p * tok : (p + 1) * tok, 128:] = value
    facts = jnp.where(lax.broadcasted_iota(jnp.int32, (16, 256), 0) == 0, facts, 0.0).astype(bf16)
    facts_ref[...] = facts
    for c in range(first_ref.shape[0]):
        first_ref[c, prompts * tok :] = facts


def make_pack(cache, rewards, assign, kgain, mine, chips):
    prompts, tok, _ = cache.shape
    smem, vmem = pl.BlockSpec(memory_space=pltpu.SMEM), pl.BlockSpec(memory_space=pltpu.VMEM)
    return pl.pallas_call(
        pack,
        in_specs=[vmem, smem, smem, vmem, vmem, smem],
        out_specs=[vmem, vmem, vmem],
        out_shape=[
            jax.ShapeDtypeStruct((chips, prompts * tok + 16, 256), bf16),
            jax.ShapeDtypeStruct((prompts * tok, 256), bf16),
            jax.ShapeDtypeStruct((16, 256), bf16),
        ],
        name="pack",
    )(cache, rewards, assign, kgain, frequency, mine)


def global_scale(sums_ref, count):
    return 1.0 / jnp.sqrt(sums_ref[0:1, 0:1] / count + spread_eps)


def rescale(dq_ref, dw0_ref, dw1_ref, sums_ref, stat_ref, dq_out, dw_out, *, count):
    r = pl.program_id(0)
    adv = jnp.where(r == 0, stat_ref[0:1, 1:2], stat_ref[0:1, 2:3]) * global_scale(sums_ref, count)
    dq_out[...] = (dq_ref[...].astype(f32) * adv).astype(bf16)
    for n, part in enumerate((dw0_ref, dw1_ref)):
        for c in range(2):
            dw_out[0, :, (2 * c + n) * 128 : (2 * c + n + 1) * 128] = (part[0, :, c * 128 : (c + 1) * 128] * adv).astype(bf16)


def make_rescale(dq, dw0, dw1, sums, stat, count):
    rolls, win, width = dq.shape
    half = pl.BlockSpec((1, win, 256), lambda r: (r, 0, 0))
    qspec = pl.BlockSpec((1, win, width), lambda r: (r, 0, 0))
    return pl.pallas_call(
        functools.partial(rescale, count=count),
        grid=(rolls,),
        in_specs=[
            qspec,
            half,
            half,
            pl.BlockSpec((8, 128), lambda r: (0, 0)),
            pl.BlockSpec((8, 128), lambda r: (0, 0)),
        ],
        out_specs=[qspec, pl.BlockSpec((1, win, 512), lambda r: (r, 0, 0))],
        out_shape=[jax.ShapeDtypeStruct(dq.shape, bf16), jax.ShapeDtypeStruct((rolls, win, 512), bf16)],
        input_output_aliases={0: 0},
        compiler_params=pltpu.CompilerParams(vmem_limit_bytes=LIMIT - 3 * 1024 * 1024),
        name="rescale",
    )(dq, dw0, dw1, sums, stat)


def merge(own0, far0, own1, far1, stat_ref, there_ref, out_ref, sums_ref):
    rows = own0.shape[1]
    for h, (own, far) in enumerate(((own0, far0), (own1, far1))):
        out_ref[:, h * rows : (h + 1) * rows] = (own[...].astype(f32) + far[...].astype(f32)).astype(bf16)
    sums_ref[...] = stat_ref[...] + there_ref[...]


def make_merge(own0, far0, own1, far1, stat, there):
    chips, rows, width = own0.shape
    whole = pl.BlockSpec((chips, rows, width), lambda i: (0, 0, 0))
    small = pl.BlockSpec((8, 128), lambda i: (0, 0))
    return pl.pallas_call(
        merge,
        grid=(1,),
        in_specs=[whole] * 4 + [small] * 2,
        out_specs=[pl.BlockSpec((chips, 2 * rows, width), lambda i: (0, 0, 0)), small],
        out_shape=[jax.ShapeDtypeStruct((chips, 2 * rows, width), bf16), jax.ShapeDtypeStruct(stat.shape, f32)],
        compiler_params=pltpu.CompilerParams(vmem_limit_bytes=LIMIT - 2 * 1024 * 1024),
        name="merge",
    )(own0, far0, own1, far1, stat, there)


def settle(d_ref, cache_ref, kg_ref, freq_ref, mine_ref, sums_ref, out_ref, *, count):
    prompts, tok, width = cache_ref.shape
    scale = global_scale(sums_ref, count)
    _, mean = helpers()
    cos, sin = turns(mine_ref[0] * tok, tok, freq_ref[...])
    for h in range(width // 256):
        for p in range(prompts):
            cut = slice((h * prompts + p) * tok, (h * prompts + p + 1) * tok)
            g = d_ref[0, cut].astype(f32)
            for m in range(1, d_ref.shape[0]):
                g += d_ref[m, cut].astype(f32)
            g *= scale
            key = pull(cache_ref[p, :, h * 128 : (h + 1) * 128], g[:, :128], pltpu.roll(g[:, :128], 64, 1), kg_ref[...], cos, sin, mean)
            out_ref[p, :, h * 128 : (h + 1) * 128] = key.astype(bf16)
            out_ref[p, :, (2 + h) * 128 : (3 + h) * 128] = g[:, 128:].astype(bf16)


def make_settle(d, cache, kgain, mine, sums, count):
    smem, vmem = pl.BlockSpec(memory_space=pltpu.SMEM), pl.BlockSpec(memory_space=pltpu.VMEM)
    return pl.pallas_call(
        functools.partial(settle, count=count),
        grid=(1,),
        in_specs=[vmem, vmem, vmem, vmem, smem, vmem],
        out_specs=vmem,
        out_shape=jax.ShapeDtypeStruct(cache.shape, bf16),
        compiler_params=pltpu.CompilerParams(vmem_limit_bytes=16 * 1024 * 1024),
        name="settle",
    )(d, cache, kgain, frequency, mine, sums)


def local(prompt_cache, key_gain, query_gain, window_cache, queries, upstream, rewards, assign, offsets):
    groups, members = lax.axis_size("prompt"), lax.axis_size("roll")
    rolls = queries.shape[0]
    prompts, tok, _ = prompt_cache.shape
    chips = members // 2
    mine = lax.axis_index("roll")
    same_core = [[2 * c + k for c in range(chips)] for k in range(2)]
    other_core = [(m, m ^ 1) for m in range(members)]

    def flip(x):
        return lax.ppermute(x, "roll", other_core)

    def far(x, step):
        return lax.ppermute(x, "prompt", [(i, i ^ step) for i in range(groups)])

    mine = mine.astype(jnp.int32)[None]
    qgain, kgain = query_gain[None], key_gain[None]
    first, second, facts = make_pack(prompt_cache, rewards, assign, kgain, mine, chips)
    ga = lax.all_to_all(first, "roll", 0, 0, tiled=True, axis_index_groups=same_core)
    scalar = jnp.concatenate([assign, mine % 2])
    qs, cw, sw, copies = make_ready(queries, qgain, offsets, second, facts, far(facts, 1), members * tok, members)
    ga, qs, cw, sw, scalar = lax.optimization_barrier((ga, qs, cw, sw, scalar))
    gb = flip(ga)
    copies, _ = lax.optimization_barrier((copies, ga))
    g1 = lax.all_to_all(copies, "roll", 0, 0, tiled=True).reshape(chips, 2, prompts * tok + 16, 256)

    def attention(h, a, b, *before):
        return call(
            h, 2, 1024, scalar, qs, queries, upstream, a, b, window_cache, qgain, kgain, cw, sw, rewards, tok, prompts, *before
        )

    att, dq, dw0, _, own0, other0 = attention(0, ga, gb)
    att, dq, dw1, stat, own1, other1 = attention(1, g1, g1, att, dq)
    merged, sums = make_merge(own0, flip(other0), own1, flip(other1), stat, far(stat, groups // 2))
    parts = lax.all_to_all(merged, "roll", 0, 0, tiled=True, axis_index_groups=same_core)
    step = 2
    while step < groups // 2:
        sums = sums + far(sums, step)
        step *= 2
    count = groups * members * rolls
    dq, window_grad = make_rescale(dq, dw0, dw1, sums, stat, count)
    prompt_grad = make_settle(parts, prompt_cache, kgain, mine, sums, count)
    return att, dq, window_grad, prompt_grad


def solution(mesh):
    both = P(("prompt", "roll"))
    return jax.shard_map(
        local,
        mesh=mesh,
        in_specs=(P("prompt", "roll", None), P(), P(), both, both, both, both, both, both),
        out_specs=(both, both, both, P("prompt", "roll", None)),
        check_vma=False,
    )
```
